256 devices in a mesh: fsdp: 32 (over x_lo, z, core), ctx: 8 (over y, x_hi).
Axes of the slice: x: 4 (x_hi: 2, x_lo: 2; x = x_hi * 2 + x_lo), y: 4, z: 8, core: 2. Of those that a mesh axis runs over, the one named last changes fastest.
Arguments:
- tokens: bfloat16 [32, 4096, 4096], P('fsdp', 'ctx'), may hold values from -24 to 24
- w_query: bfloat16 [4096, 2, 128], P('fsdp'), may hold values from -0.09375 to 0.09375
- w_key: bfloat16 [4096, 2, 128], P('fsdp'), may hold values from -0.09375 to 0.09375
- w_value: bfloat16 [4096, 2, 4, 128], P('fsdp'), may hold values from -0.09375 to 0.09375
- w_out: bfloat16 [2, 4, 128, 4096], P(None, None, None, 'fsdp'), may hold values from -0.5 to 0.5
- value_experts: int32 [32, 4096, 2, 2], P('fsdp', 'ctx'), may hold values from 0 to 3, all different within a row
- value_gates: bfloat16 [32, 4096, 2, 2], P('fsdp', 'ctx'), may hold values from 0.25 to 1
- output_experts: int32 [32, 4096, 2, 2], P('fsdp', 'ctx'), may hold values from 0 to 3, all different within a row
- output_gates: bfloat16 [32, 4096, 2, 2], P('fsdp', 'ctx'), may hold values from 0.25 to 1
Outputs:
- projected: bfloat16 [32, 4096, 4096], P('fsdp', 'ctx')
The draws below stay inside these ranges and needn't reach their ends.
Inputs may be any that keep to these rules, and one draw needn't show every extreme that they name: `value_experts`: each token and head names 2 different experts. `output_experts`: each token and head names 2 different experts.
All inputs are finite; a program needn't handle non-finite values.
Results may differ from the reference program's by a relative error of at most 0.015.
The reference program's roundings to bfloat16 on the way (of `queries`, `key_rows`, `value_rows`, `weights`, `attended`, `output_mix` and `mixed_in`) count: a program that leaves them out, or rounds other values in their place, can miss the bound.
Values may be sent and summed in bfloat16 or wider, within the bound.
No kernel may reach another device: no remote copies, remote signals or barrier semaphores. Data moves between devices by JAX's collectives and lax.ppermute only.
A program may use at most 128 MiB of HBM per device.

```python
import math
import jax
import jax.numpy as jnp
from jax import lax

D = 4096
DH = 128
HEADS = 2
EXPERTS = 4
TOP = 2
SEQS = 32
LEN = 4096


def draw_tokens(key, part):
    first = jax.random.fold_in(jax.random.fold_in(key, 11), 0)
    base = jax.random.normal(first, (SEQS, LEN, D), jnp.float32)
    return jnp.clip(base, -6.0, 6.0).astype(jnp.bfloat16)


def block_levels(key, dims, cuts, smallest, largest):
    def one(dim, parts):
        steps = jax.random.uniform(jax.random.fold_in(jax.random.fold_in(key, 6), dim), (parts,), jnp.float32, smallest / len(cuts), largest / len(cuts))
        return jnp.repeat(jnp.exp(steps), dims[dim] // parts).reshape((-1,) + (1,) * (len(dims) - dim - 1))

    loudness = one(*cuts[0])
    for cut in cuts[1:]:
        loudness = loudness * one(*cut)
    return loudness


def choose_distinct(own_key, rows, count, top, lift):
    order = jax.random.permutation(jax.random.fold_in(own_key, 1), count)
    favour = order
    for power in range(3):
        favour = favour * favour // count
    favour = favour * lift // count
    tickets = jax.random.randint(jax.random.fold_in(own_key, 2), (rows, count), 0, 4096) + favour
    sure = jax.random.permutation(jax.random.fold_in(own_key, 3), rows)[jnp.arange(count) % rows]
    tickets = jnp.where(jnp.arange(rows)[:, None] == sure[None, :], 1 << 14, tickets)
    score = tickets * count + jnp.arange(count)
    return lax.top_k(score.astype(jnp.int32), top)[1].astype(jnp.int32)


def noise(own_key, extent, scale, limit, shards=(), kind=jnp.bfloat16):
    factor_of = block_levels(own_key, extent, shards, -0.22, 0.18) if shards else 1.0
    values = jax.random.normal(own_key, extent, jnp.float32) * scale * factor_of
    return jnp.minimum(jnp.maximum(values, -limit), limit).astype(kind)


def setup_inputs(seed: int = 0) -> dict:
    keys = jax.random.split(jax.random.key(seed), 10)
    tokens = draw_tokens(jax.random.fold_in(keys[9], 71), 0)
    w_query = noise(keys[1], (D, HEADS, DH), D ** -0.5, 0.09375, ((0, 32),))
    w_key = noise(keys[2], (D, HEADS, DH), D ** -0.5, 0.09375, ((0, 32),))
    w_value = noise(keys[3], (D, HEADS, EXPERTS, DH), D ** -0.5, 0.09375, ((0, 32),))
    w_out = noise(keys[4], (HEADS, EXPERTS, DH, D), DH ** -0.5, 0.5, ((3, 32),))
    value_experts = choose_distinct(keys[5], SEQS * LEN * HEADS, EXPERTS, TOP, 4096).reshape((SEQS, LEN, HEADS, TOP))
    value_gates = jnp.clip(0.25 + 0.75 * jax.random.uniform(keys[6], (SEQS, LEN, HEADS, TOP), jnp.float32) ** block_levels(keys[6], (SEQS, LEN, HEADS, TOP), ((0, 32), (1, 8)), -0.2, 0.2), 0.25, 1.0).astype(jnp.bfloat16)
    output_experts = choose_distinct(keys[7], SEQS * LEN * HEADS, EXPERTS, TOP, 4096).reshape((SEQS, LEN, HEADS, TOP))
    output_gates = jnp.clip(0.25 + 0.75 * jax.random.uniform(keys[8], (SEQS, LEN, HEADS, TOP), jnp.float32) ** block_levels(keys[8], (SEQS, LEN, HEADS, TOP), ((0, 32), (1, 8)), -0.2, 0.2), 0.25, 1.0).astype(jnp.bfloat16)
    return dict(tokens=tokens, w_query=w_query, w_key=w_key, w_value=w_value, w_out=w_out, value_experts=value_experts, value_gates=value_gates, output_experts=output_experts, output_gates=output_gates)


def expert_mix(indices, gates, experts):
    one_hot = (indices[..., None] == jnp.arange(experts, dtype=jnp.int32)).astype(jnp.float32)
    return lax.optimization_barrier(jnp.sum(gates.astype(jnp.float32)[..., None] * one_hot, axis=-2))

def settle(values):
    return lax.optimization_barrier(values.astype(jnp.bfloat16)).astype(jnp.float32)

def reference(tokens, w_query, w_key, w_value, w_out, value_experts, value_gates, output_experts, output_gates):

    def one_sequence(bundle):
        sequence, value_ids, value_wts, output_ids, output_wts = bundle
        queries = settle(jnp.dot(sequence, w_query.reshape(D, HEADS * DH), preferred_element_type=jnp.float32)).reshape(LEN, HEADS, DH)
        key_rows = settle(jnp.dot(sequence, w_key.reshape(D, HEADS * DH), preferred_element_type=jnp.float32)).reshape(LEN, HEADS, DH)
        experts_out = jnp.dot(sequence, w_value.reshape(D, HEADS * EXPERTS * DH), preferred_element_type=jnp.float32).reshape(LEN, HEADS, EXPERTS, DH)
        value_mix = expert_mix(value_ids, value_wts, EXPERTS)
        value_rows = settle(lax.optimization_barrier(jnp.sum(value_mix[..., None] * experts_out, axis=2)))
        scores = jnp.einsum('qhd,khd->hqk', queries, key_rows) / math.sqrt(DH)
        positions = jnp.arange(LEN, dtype=jnp.int32)
        causal = positions[:, None] >= positions[None, :]
        scores = jnp.where(causal[None], scores, -jnp.inf)
        peak = lax.optimization_barrier(jnp.max(scores, axis=-1, keepdims=True))
        weights = jnp.exp(scores - peak)
        total = lax.optimization_barrier(jnp.sum(weights, axis=-1))
        summed = jnp.einsum('hqk,khd->qhd', settle(weights), value_rows)
        attended = settle(summed / jnp.transpose(total)[:, :, None])
        output_mix = settle(expert_mix(output_ids, output_wts, EXPERTS))
        mixed_in = (output_mix[..., None] * attended[:, :, None, :]).astype(jnp.bfloat16)
        result = jnp.dot(mixed_in.reshape(LEN, HEADS * EXPERTS * DH), w_out.reshape(HEADS * EXPERTS * DH, D), preferred_element_type=jnp.float32)
        return result.astype(jnp.bfloat16)
    return lax.map(one_sequence, (tokens, value_experts, value_gates, output_experts, output_gates))
```

```python
import functools
import math

import jax
import jax.numpy as jnp
from jax import lax
from jax.experimental import pallas as pl
from jax.experimental.pallas import tpu as pltpu
from jax.sharding import Mesh
from jax.sharding import PartitionSpec as P

AXES = ("x_lo", "z", "core", "y", "x_hi")
SIZES = (2, 8, 2, 4, 2)
FSDP = ("x_lo", "z", "core")
CTX = ("y", "x_hi")
HEADS, EXPERTS, DH = 2, 4, 128
WIDTH = HEADS * DH
MIB = 1 << 20


def expert_mix(indices, gates):
    one_hot = (indices[..., None] == jnp.arange(EXPERTS, dtype=jnp.int32)).astype(jnp.float32)
    mix = jnp.sum(gates.astype(jnp.float32)[..., None] * one_hot, axis=-2)
    return mix.reshape(mix.shape[0], HEADS * EXPERTS)


def project_kernel(x_ref, w_ref, mix_ref, q_ref, kv_ref, acc_ref):
    n = pl.program_id(0)
    block = jnp.dot(x_ref[...], w_ref[...], preferred_element_type=jnp.float32)

    @pl.when(n == 0)
    def _():
        q_ref[...] = block.astype(jnp.bfloat16)

    @pl.when(n == 1)
    def _():
        kv_ref[:, :WIDTH] = block.astype(jnp.bfloat16)

    for head in range(HEADS):
        for half in range(2):

            @pl.when(n == 2 + 2 * head + half)
            def _():
                first = head * EXPERTS + 2 * half
                part = (
                    mix_ref[:, first : first + 1] * block[:, :DH]
                    + mix_ref[:, first + 1 : first + 2] * block[:, DH:]
                )
                if half == 0:
                    acc_ref[...] = part
                else:
                    start = WIDTH + head * DH
                    kv_ref[:, start : start + DH] = (acc_ref[...] + part).astype(jnp.bfloat16)


def project(x, w, mix):
    rows, depth = x.shape
    columns = w.shape[1]
    return pl.pallas_call(
        project_kernel,
        grid=(columns // WIDTH,),
        in_specs=[
            pl.BlockSpec((rows, depth), lambda n: (0, 0)),
            pl.BlockSpec((depth, WIDTH), lambda n: (0, n)),
            pl.BlockSpec((rows, HEADS * EXPERTS), lambda n: (0, 0)),
        ],
        out_specs=[
            pl.BlockSpec((rows, WIDTH), lambda n: (0, 0)),
            pl.BlockSpec((rows, 2 * WIDTH), lambda n: (0, 0)),
        ],
        out_shape=[
            jax.ShapeDtypeStruct((rows, WIDTH), jnp.bfloat16),
            jax.ShapeDtypeStruct((rows, 2 * WIDTH), jnp.bfloat16),
        ],
        scratch_shapes=[pltpu.VMEM((rows, DH), jnp.float32)],
        compiler_params=pltpu.CompilerParams(vmem_limit_bytes=40 * MIB),
        cost_estimate=pl.CostEstimate(
            flops=2 * rows * depth * columns,
            bytes_accessed=2 * (rows * depth + depth * columns),
            transcendentals=0,
        ),
    )(x, w, mix)


def attend_kernel(count, place_ref, q_ref, mix_ref, *refs):
    kv_refs, out_ref = refs[:count], refs[count]
    m_ref, l_ref, acc_ref = refs[count + 1 :]
    place = place_ref[0]
    rows = q_ref.shape[0]
    scale = 1.0 / math.sqrt(DH)
    for head in range(HEADS):
        lanes = slice(head * DH, (head + 1) * DH)

        def step(k, lanes=lanes, head=head):
            kv = kv_refs[k]
            scores = (
                lax.dot_general(
                    q_ref[:, lanes],
                    kv[:, lanes],
                    (((1,), (1,)), ((), ())),
                    preferred_element_type=jnp.float32,
                )
                * scale
            )
            values = kv[:, WIDTH + head * DH : WIDTH + (head + 1) * DH]
            if k == 0:
                q_pos = lax.broadcasted_iota(jnp.int32, scores.shape, 0)
                k_pos = lax.broadcasted_iota(jnp.int32, scores.shape, 1)
                scores = jnp.where(q_pos >= k_pos, scores, -jnp.inf)
                top = jnp.max(scores, axis=1, keepdims=True)
                weights = jnp.exp(scores - top)
                m_ref[head] = top
                l_ref[head] = jnp.sum(weights, axis=1, keepdims=True)
                acc_ref[:, lanes] = jnp.dot(
                    weights.astype(jnp.bfloat16), values, preferred_element_type=jnp.float32
                )
            else:
                before = m_ref[head]
                top = jnp.maximum(before, jnp.max(scores, axis=1, keepdims=True))
                rescale = jnp.exp(before - top)
                weights = jnp.exp(scores - top)
                m_ref[head] = top
                l_ref[head] = l_ref[head] * rescale + jnp.sum(weights, axis=1, keepdims=True)
                acc_ref[:, lanes] = acc_ref[:, lanes] * rescale + jnp.dot(
                    weights.astype(jnp.bfloat16), values, preferred_element_type=jnp.float32
                )

        for k in range(count):
            if k == 0:
                step(0)
            else:
                pl.when(place >= k)(functools.partial(step, k))
        attended = (acc_ref[:, lanes] / l_ref[head]).astype(jnp.bfloat16).astype(jnp.float32)
        for expert in range(EXPERTS):
            index = head * EXPERTS + expert
            out_ref[:, index * DH : (index + 1) * DH] = (
                mix_ref[:, index : index + 1] * attended
            ).astype(jnp.bfloat16)


def attend(place, q, mix, blocks):
    rows = q.shape[0]
    count = len(blocks)
    return pl.pallas_call(
        functools.partial(attend_kernel, count),
        in_specs=[pl.BlockSpec(memory_space=pltpu.SMEM)]
        + [pl.BlockSpec(memory_space=pltpu.VMEM)] * (2 + count),
        out_specs=pl.BlockSpec(memory_space=pltpu.VMEM),
        out_shape=jax.ShapeDtypeStruct((rows, HEADS * EXPERTS * DH), jnp.bfloat16),
        scratch_shapes=[
            pltpu.VMEM((HEADS, rows, 1), jnp.float32),
            pltpu.VMEM((HEADS, rows, 1), jnp.float32),
            pltpu.VMEM((rows, WIDTH), jnp.float32),
        ],
        compiler_params=pltpu.CompilerParams(vmem_limit_bytes=40 * MIB),
        cost_estimate=pl.CostEstimate(
            flops=4 * rows * rows * DH * HEADS * count,
            bytes_accessed=2 * rows * WIDTH * 2 * count,
            transcendentals=rows * rows * HEADS * count,
        ),
    )(place, q, mix, *blocks)


PANELS = 4


def output_kernel(a_ref, w_ref, o_ref):
    panel = jnp.concatenate([w_ref[i] for i in range(PANELS)], axis=1)
    o_ref[...] = jnp.dot(a_ref[...], panel, preferred_element_type=jnp.float32).astype(jnp.bfloat16)


def output(mixed, panels):
    rows, depth = mixed.shape
    count, _, width = panels.shape
    return pl.pallas_call(
        output_kernel,
        grid=(count // PANELS,),
        in_specs=[
            pl.BlockSpec((rows, depth), lambda n: (0, 0)),
            pl.BlockSpec((PANELS, depth, width), lambda n: (n, 0, 0)),
        ],
        out_specs=pl.BlockSpec((rows, PANELS * width), lambda n: (0, n)),
        out_shape=jax.ShapeDtypeStruct((rows, count * width), jnp.bfloat16),
        compiler_params=pltpu.CompilerParams(vmem_limit_bytes=40 * MIB),
        cost_estimate=pl.CostEstimate(
            flops=2 * rows * depth * count * width,
            bytes_accessed=2 * (rows * count * width + depth * count * width),
            transcendentals=0,
        ),
    )(mixed, panels)


def on_device(
    tokens, w_query, w_key, w_value, w_out, value_experts, value_gates, output_experts, output_gates
):
    x = tokens[0]
    shard = w_query.shape[0]
    w_all = jnp.concatenate(
        [w.reshape(shard, -1) for w in (w_query, w_key, w_value)], axis=1
    )
    w_all = lax.all_gather(w_all, FSDP, axis=0, tiled=True)
    panel = w_out.reshape(-1, w_out.shape[3])
    panels = lax.all_gather(panel, FSDP, axis=0, tiled=False)
    value_mix = expert_mix(value_experts[0], value_gates[0])
    output_mix = expert_mix(output_experts[0], output_gates[0])
    output_mix = output_mix.astype(jnp.bfloat16).astype(jnp.float32)
    q, kv = project(x, w_all, value_mix)
    count = lax.axis_size(CTX)
    place = lax.axis_index(CTX)
    blocks = [kv] + [
        lax.ppermute(kv, CTX, [(i, i + k) for i in range(count - k)]) for k in range(1, count)
    ]
    mixed = attend(place.astype(jnp.int32).reshape(1), q, output_mix, blocks)
    return output(mixed, panels)[None]


def solution(mesh):
    grid = Mesh(mesh.devices.reshape(SIZES), AXES)
    seq = P(FSDP, CTX, None, None)
    in_specs = (
        P(FSDP, CTX, None),
        P(FSDP, None, None),
        P(FSDP, None, None),
        P(FSDP, None, None, None),
        P(None, None, None, FSDP),
        seq,
        seq,
        seq,
        seq,
    )
    return jax.shard_map(
        on_device, mesh=grid, in_specs=in_specs, out_specs=P(FSDP, CTX, None), check_vma=False
    )
```

```python
import functools
import itertools
import math

import jax
import jax.numpy as jnp
from jax import lax
from jax.experimental import pallas as pl
from jax.experimental.pallas import tpu as pltpu
from jax.sharding import Mesh
from jax.sharding import PartitionSpec as P

AXES = ("x_lo", "z", "core", "y", "x_hi")
SIZES = (2, 8, 2, 4, 2)
FSDP = ("x_lo", "z", "core")
CTX = ("y", "x_hi")
HEADS, EXPERTS, DH = 2, 4, 128
WIDTH = HEADS * DH
MIB = 1 << 20


def expert_mix(indices, gates):
    one_hot = (indices[..., None] == jnp.arange(EXPERTS, dtype=jnp.int32)).astype(jnp.float32)
    mix = jnp.sum(gates.astype(jnp.float32)[..., None] * one_hot, axis=-2)
    return mix.reshape(mix.shape[0], HEADS * EXPERTS)


SLICE = 16
RING = 4
VM = pltpu.CompilerParams(vmem_limit_bytes=60 * MIB)


def moved(x, target):
    pairs = []
    for source, (x_lo, z, core, y, x_hi) in enumerate(itertools.product(*map(range, SIZES))):
        to_x, to_y, to_core = target(2 * x_hi + x_lo, y, core)
        to_x, to_y = to_x % RING, to_y % RING
        place = (((to_x % 2) * SIZES[1] + z) * SIZES[2] + to_core) * SIZES[3] + to_y
        pairs.append((source, place * SIZES[4] + to_x // 2))
    return lax.ppermute(x, AXES, pairs)


def hop(x, by, phase):
    return moved(
        x, lambda cx, cy, core: (cx + by, cy, core) if core == phase else (cx, cy + by, core)
    )


def swapped(x):
    return lax.ppermute(x, "core", [(0, 1), (1, 0)])


SHIFTS = (0, 4, 3, -3, 2, -2, 1, -1)
FIRST = ((0, -1), (1, 2))
GROUPS = ((0, 0), (0, 1), (-1, 0), (1, 1), (1, 0), (-1, 1), (2, 0), (2, 1))


def gathered(w):
    count = SIZES[1]
    which = lax.axis_index("y") * SIZES[4] + lax.axis_index("x_hi")
    own = lax.dynamic_slice_in_dim(w, which * SLICE, SLICE, axis=0)
    block = jnp.stack(
        [own]
        + [
            lax.ppermute(own, "z", [(i, (i + by) % count) for i in range(count)])
            for by in SHIFTS[1:]
        ]
    )
    up = hop(block, 1, 0)
    down = hop(block, -1, 0)
    across = hop(block, 2, 0)
    near = jnp.stack([block, up])
    far = jnp.stack([down, across])
    near_up = hop(near, 1, 1)
    far_down = hop(far, -1, 1)
    near_down = hop(near, -1, 1)
    far_up = hop(far, 1, 1)
    near_across = hop(near_up, 1, 1)
    far_across = hop(far_down, -1, 1)
    held = [near, far, near_up, far_down, near_down, far_up, near_across, far_across]
    return held + [swapped(h) for h in held]


def project_kernel(count, place_ref, x_hbm, mix_ref, *refs):
    pieces = refs[:count]
    kv_ref = refs[count]
    x_ref, w_ref, x_sem, k_sem, v_sem = refs[count + 1 :]
    rows = x_ref.shape[0]
    width = SIZES[2] * 8 * SLICE
    chip_x, chip_y, level, core = (place_ref[i] for i in range(4))
    copies = []
    for lo in range(SIZES[0]):
        for k, by in enumerate(SHIFTS):
            column = lo * SIZES[1] + lax.rem(level - by + SIZES[1], SIZES[1])
            copies.append(
                pltpu.make_async_copy(
                    x_hbm.at[:, pl.ds(pl.multiple_of(column * width, width), width)],
                    x_ref.at[:, pl.ds((lo * SIZES[1] + k) * width, width)],
                    x_sem,
                )
            )
    k_copies, v_copies = [], []
    for i in range(count):
        second, group = GROUPS[i % len(GROUPS)]
        owner = core if i < len(GROUPS) else 1 - core
        for j, first in enumerate(FIRST[group]):
            by_x = jnp.where(owner == 0, first, second)
            by_y = jnp.where(owner == 0, second, first)
            from_x = lax.rem(chip_x + by_x + RING, RING)
            from_y = lax.rem(chip_y + by_y + RING, RING)
            part = from_y * SIZES[4] + lax.div(from_x, 2)
            for columns, sem, into in (
                (slice(0, WIDTH), k_sem, k_copies),
                (slice(WIDTH, WIDTH + WIDTH * EXPERTS), v_sem, v_copies),
            ):
                into.append(
                    pltpu.make_async_copy(
                        pieces[i].at[j, :, :, columns],
                        w_ref.at[lax.rem(from_x, 2), :, owner, part, :, columns],
                        sem,
                    )
                )
    for copy in k_copies + copies + v_copies:
        copy.start()
    for copy in k_copies + copies:
        copy.wait()

    def product(column, size):
        w = w_ref[:, :, :, :, :, column : column + size].reshape(x_ref.shape[1], size)
        return jnp.dot(x_ref[...], w, preferred_element_type=jnp.float32)

    kv_ref[:, :WIDTH] = product(0, WIDTH).astype(jnp.bfloat16)
    for copy in v_copies:
        copy.wait()
    for head in range(HEADS):
        total = None
        for half in range(2):
            expert = head * EXPERTS + 2 * half
            block = product(WIDTH + expert * DH, 2 * DH)
            part = (
                mix_ref[:, expert : expert + 1] * block[:, :DH]
                + mix_ref[:, expert + 1 : expert + 2] * block[:, DH:]
            )
            total = part if total is None else total + part
        start = WIDTH + head * DH
        kv_ref[:, start : start + DH] = total.astype(jnp.bfloat16)


def project(place, x, mix, pieces):
    rows, depth = x.shape
    columns = pieces[0].shape[-1]
    count = len(pieces)
    any_space = pl.BlockSpec(memory_space=pl.ANY)
    vmem = pl.BlockSpec(memory_space=pltpu.VMEM)
    return pl.pallas_call(
        functools.partial(project_kernel, count),
        in_specs=[pl.BlockSpec(memory_space=pltpu.SMEM), any_space, vmem] + [any_space] * count,
        out_specs=vmem,
        out_shape=jax.ShapeDtypeStruct((rows, 2 * WIDTH), jnp.bfloat16),
        scratch_shapes=[
            pltpu.VMEM((rows, depth), jnp.bfloat16),
            pltpu.VMEM((SIZES[0], SIZES[1], SIZES[2], 8, SLICE, columns), jnp.bfloat16),
            pltpu.SemaphoreType.DMA,
            pltpu.SemaphoreType.DMA,
            pltpu.SemaphoreType.DMA,
        ],
        compiler_params=VM,
        cost_estimate=pl.CostEstimate(
            flops=2 * rows * depth * columns,
            bytes_accessed=2 * (rows * depth + depth * columns),
            transcendentals=0,
        ),
    )(place, x, mix, *pieces)


def query_kernel(x_ref, w_ref, q_ref, acc_ref):
    n = pl.program_id(0)
    count = w_ref.shape[0]
    w = jnp.concatenate(
        [
            jnp.concatenate([w_ref[i, :DH], w_ref[i, DH:]], axis=1)
            for i in range(count)
        ],
        axis=0,
    )
    part = jnp.dot(x_ref[...], w, preferred_element_type=jnp.float32)

    @pl.when(n == 0)
    def _():
        acc_ref[...] = part

    @pl.when(n > 0)
    def _():
        acc_ref[...] += part

    @pl.when(n == pl.num_programs(0) - 1)
    def _():
        q_ref[...] = acc_ref[...].astype(jnp.bfloat16)


def query(x, panels):
    rows, depth = x.shape
    shards = panels.shape[0]
    steps = 4
    return pl.pallas_call(
        query_kernel,
        grid=(steps,),
        in_specs=[
            pl.BlockSpec((rows, depth // steps), lambda n: (0, n)),
            pl.BlockSpec((shards // steps, WIDTH, DH), lambda n: (n, 4, 0)),
        ],
        out_specs=pl.BlockSpec((rows, WIDTH), lambda n: (0, 0)),
        out_shape=jax.ShapeDtypeStruct((rows, WIDTH), jnp.bfloat16),
        scratch_shapes=[pltpu.VMEM((rows, WIDTH), jnp.float32)],
        compiler_params=VM,
        cost_estimate=pl.CostEstimate(
            flops=2 * rows * depth * WIDTH,
            bytes_accessed=2 * (rows * depth + depth * WIDTH),
            transcendentals=0,
        ),
    )(x, panels)


LOG2E = 1.4426950408889634


def attend_kernel(first, last, count, flag_ref, q_ref, *refs):
    refs = list(refs)
    if not first:
        state_in = [refs.pop(0) for _ in range(3)]
    if last:
        mix_ref = refs.pop(0)
    kv_refs = [refs.pop(0) for _ in range(count)]
    if last:
        out_ref = refs.pop(0)
    m_ref, l_ref, acc_ref = refs
    scale = LOG2E / math.sqrt(DH)
    for head in range(HEADS):
        lanes = slice(head * DH, (head + 1) * DH)
        if not first:
            m_ref[head] = state_in[0][head]
            l_ref[head] = state_in[1][head]
            acc_ref[:, lanes] = state_in[2][:, lanes]

        def step(k, lanes=lanes, head=head):
            kv = kv_refs[k]
            scores = lax.dot_general(
                q_ref[:, lanes],
                kv[:, lanes],
                (((1,), (1,)), ((), ())),
                preferred_element_type=jnp.float32,
            )
            values = kv[:, WIDTH + head * DH : WIDTH + (head + 1) * DH]
            if first and k == 0:
                q_pos = lax.broadcasted_iota(jnp.int32, scores.shape, 0)
                k_pos = lax.broadcasted_iota(jnp.int32, scores.shape, 1)
                scores = jnp.where(q_pos >= k_pos, scores, -jnp.inf)
                top = jnp.max(scores, axis=1, keepdims=True)
                weights = jnp.exp2((scores - top) * scale)
                m_ref[head] = top
                l_ref[head] = jnp.sum(weights, axis=1, keepdims=True)
                acc_ref[:, lanes] = jnp.dot(
                    weights.astype(jnp.bfloat16), values, preferred_element_type=jnp.float32
                )
            else:
                before = m_ref[head]
                top = jnp.maximum(before, jnp.max(scores, axis=1, keepdims=True))
                rescale = jnp.exp2((before - top) * scale)
                weights = jnp.exp2((scores - top) * scale)
                m_ref[head] = top
                l_ref[head] = l_ref[head] * rescale + jnp.sum(weights, axis=1, keepdims=True)
                acc_ref[:, lanes] = acc_ref[:, lanes] * rescale + jnp.dot(
                    weights.astype(jnp.bfloat16), values, preferred_element_type=jnp.float32
                )

        for k in range(count):
            if first and k == 0:
                step(0)
            else:
                pl.when(flag_ref[k] > 0)(functools.partial(step, k))
        if last:
            attended = (acc_ref[:, lanes] / l_ref[head]).astype(jnp.bfloat16).astype(jnp.float32)
            for expert in range(EXPERTS):
                index = head * EXPERTS + expert
                out_ref[:, index * DH : (index + 1) * DH] = (
                    mix_ref[:, index : index + 1] * attended
                ).astype(jnp.bfloat16)


def attend(flags, q, blocks, state=None, mix=None):
    rows = q.shape[0]
    count = len(blocks)
    first, last = state is None, mix is not None
    shapes = [
        jax.ShapeDtypeStruct((HEADS, rows, 1), jnp.float32),
        jax.ShapeDtypeStruct((HEADS, rows, 1), jnp.float32),
        jax.ShapeDtypeStruct((rows, WIDTH), jnp.float32),
    ]
    operands = [flags, q] + ([] if first else list(state)) + ([mix] if last else []) + list(blocks)
    vmem = pl.BlockSpec(memory_space=pltpu.VMEM)
    return pl.pallas_call(
        functools.partial(attend_kernel, first, last, count),
        in_specs=[pl.BlockSpec(memory_space=pltpu.SMEM)] + [vmem] * (len(operands) - 1),
        out_specs=vmem if last else [vmem] * 3,
        out_shape=jax.ShapeDtypeStruct((rows, HEADS * EXPERTS * DH), jnp.bfloat16)
        if last
        else shapes,
        scratch_shapes=[pltpu.VMEM(s.shape, s.dtype) for s in shapes] if last else [],
        compiler_params=VM,
        cost_estimate=pl.CostEstimate(
            flops=4 * rows * rows * DH * HEADS * count,
            bytes_accessed=2 * rows * WIDTH * 2 * count,
            transcendentals=rows * rows * HEADS * count,
        ),
    )(*operands)


PANELS = 4


def output_kernel(a_ref, w_ref, o_ref):
    panel = jnp.concatenate([w_ref[i] for i in range(PANELS)], axis=1)
    o_ref[...] = jnp.dot(a_ref[...], panel, preferred_element_type=jnp.float32).astype(jnp.bfloat16)


def output(mixed, panels):
    rows, depth = mixed.shape
    count, _, width = panels.shape
    return pl.pallas_call(
        output_kernel,
        grid=(count // PANELS,),
        in_specs=[
            pl.BlockSpec((rows, depth), lambda n: (0, 0)),
            pl.BlockSpec((PANELS, depth, width), lambda n: (n, 0, 0)),
        ],
        out_specs=pl.BlockSpec((rows, PANELS * width), lambda n: (0, n)),
        out_shape=jax.ShapeDtypeStruct((rows, count * width), jnp.bfloat16),
        compiler_params=VM,
        cost_estimate=pl.CostEstimate(
            flops=2 * rows * depth * count * width,
            bytes_accessed=2 * (rows * count * width + depth * count * width),
            transcendentals=0,
        ),
    )(mixed, panels)


def on_device(
    tokens, w_query, w_key, w_value, w_out, value_experts, value_gates, output_experts, output_gates
):
    x = tokens[0]
    shard = w_query.shape[0]
    y, x_hi = lax.axis_index("y"), lax.axis_index("x_hi")
    chip_x = 2 * x_hi + lax.axis_index("x_lo")
    place = jnp.stack([chip_x, y, lax.axis_index("z"), lax.axis_index("core")]).astype(jnp.int32)
    panel = jnp.concatenate(
        [
            w_out.reshape(-1, w_out.shape[3]),
            jnp.transpose(w_query, (1, 0, 2)).reshape(-1, DH),
        ],
        axis=0,
    )
    panels = lax.all_gather(panel, FSDP, axis=0, tiled=False)
    pieces = gathered(
        jnp.concatenate([w.reshape(shard, -1) for w in (w_key, w_value)], axis=1)
    )
    value_mix = expert_mix(value_experts[0], value_gates[0])
    output_mix = expert_mix(output_experts[0], output_gates[0])
    output_mix = output_mix.astype(jnp.bfloat16).astype(jnp.float32)
    own = project(place, x, value_mix, pieces)
    q = query(x, panels)

    other = lax.ppermute(own, "x_hi", [(0, 1), (1, 0)])
    own_1 = lax.ppermute(own, "y", [(0, 1), (1, 2), (2, 3)])
    own_3 = lax.ppermute(own, "y", [(0, 3)])
    own_2 = lax.ppermute(own_1, "y", [(1, 2), (2, 3)])
    other_1 = lax.ppermute(other, "y", [(0, 1), (1, 2), (2, 3)])
    other_3 = lax.ppermute(other, "y", [(0, 3)])
    other_2 = lax.ppermute(own_2, "x_hi", [(0, 1), (1, 0)])
    one = jnp.int32(1)
    flags = [x_hi, y >= 1, y >= 1, y >= 2, y >= 2, y >= 3, y >= 3]
    flags = [f.astype(jnp.int32) for f in flags]
    early = jnp.stack([one, flags[0], flags[1], flags[5]])
    late = jnp.stack([flags[2], flags[3], flags[4], flags[6]])
    state = attend(early, q, [own, other, own_1, own_3])
    mixed = attend(late, q, [other_1, own_2, other_2, other_3], state=state, mix=output_mix)
    return output(mixed, panels)[None]


def solution(mesh):
    grid = Mesh(mesh.devices.reshape(SIZES), AXES)
    seq = P(FSDP, CTX, None, None)
    in_specs = (
        P(FSDP, CTX, None),
        P(FSDP, None, None),
        P(FSDP, None, None),
        P(FSDP, None, None, None),
        P(None, None, None, FSDP),
        seq,
        seq,
        seq,
        seq,
    )
    return jax.shard_map(
        on_device, mesh=grid, in_specs=in_specs, out_specs=P(FSDP, CTX, None), check_vma=False
    )
```

```python
import functools
import itertools
import math

import jax
import jax.numpy as jnp
from jax import lax
from jax.experimental import pallas as pl
from jax.experimental.pallas import tpu as pltpu
from jax.sharding import Mesh
from jax.sharding import PartitionSpec as P

AXES = ("x_lo", "z", "core", "y", "x_hi")
SIZES = (2, 8, 2, 4, 2)
FSDP = ("x_lo", "z", "core")
CTX = ("y", "x_hi")
HEADS, EXPERTS, DH = 2, 4, 128
WIDTH = HEADS * DH
MIB = 1 << 20


def expert_mix(indices, gates):
    one_hot = (indices[..., None] == jnp.arange(EXPERTS, dtype=jnp.int32)).astype(jnp.float32)
    mix = jnp.sum(gates.astype(jnp.float32)[..., None] * one_hot, axis=-2)
    return mix.reshape(mix.shape[0], HEADS * EXPERTS).T


RING = 4
VM = pltpu.CompilerParams(vmem_limit_bytes=60 * MIB)


def moved(x, target):
    pairs = []
    for source, (x_lo, z, core, y, x_hi) in enumerate(itertools.product(*map(range, SIZES))):
        to_x, to_y, to_core = target(2 * x_hi + x_lo, y, core)
        to_x, to_y = to_x % RING, to_y % RING
        place = (((to_x % 2) * SIZES[1] + z) * SIZES[2] + to_core) * SIZES[3] + to_y
        pairs.append((source, place * SIZES[4] + to_x // 2))
    return lax.ppermute(x, AXES, pairs)


def hop(x, by, phase):
    return moved(
        x, lambda cx, cy, core: (cx + by, cy, core) if core == phase else (cx, cy + by, core)
    )


def swapped(x):
    return lax.ppermute(x, "core", [(0, 1), (1, 0)])


FIRST = ((0, -1), (1, 2))
GROUPS = ((0, 0), (0, 1), (-1, 0), (1, 1), (1, 0), (-1, 1), (2, 0), (2, 1))


def lifted(x):
    pairs = []
    for source, (x_lo, z, core, y, x_hi) in enumerate(itertools.product(*map(range, SIZES))):
        by = y * SIZES[4] + x_hi
        to_z = (z + by if core == 0 else z - by) % SIZES[1]
        place = ((x_lo * SIZES[1] + to_z) * SIZES[2] + core) * SIZES[3] + y
        pairs.append((source, place * SIZES[4] + x_hi))
    return lax.ppermute(x, AXES, pairs)


def gathered(block):
    up = hop(block, 1, 0)
    down = hop(block, -1, 0)
    across = hop(block, 2, 0)
    near = jnp.stack([block, up])
    far = jnp.stack([down, across])
    near_up = hop(near, 1, 1)
    far_down = hop(far, -1, 1)
    near_down = hop(near, -1, 1)
    far_up = hop(far, 1, 1)
    near_across = hop(near_up, 1, 1)
    far_across = hop(far_down, -1, 1)
    return [near, far, near_up, far_down, near_down, far_up, near_across, far_across]


def pack_kernel(place_ref, own_ref, other_ref, out_ref):
    rows = own_ref.shape[0]
    core = place_ref[3]
    for i in range(SIZES[0] * SIZES[1]):
        lanes = pl.ds(pl.multiple_of((SIZES[2] * i + core) * DH, DH), DH)
        out_ref[:rows, i * DH : (i + 1) * DH] = own_ref[:, lanes]
        out_ref[rows:, i * DH : (i + 1) * DH] = other_ref[:, lanes]


def packed(place, own, other):
    rows, depth = own.shape
    vmem = pl.BlockSpec(memory_space=pltpu.VMEM)
    return pl.pallas_call(
        pack_kernel,
        in_specs=[pl.BlockSpec(memory_space=pltpu.SMEM), vmem, vmem],
        out_specs=vmem,
        out_shape=jax.ShapeDtypeStruct((2 * rows, depth // 2), own.dtype),
        compiler_params=VM,
        cost_estimate=pl.CostEstimate(
            flops=0, bytes_accessed=6 * rows * depth, transcendentals=0
        ),
    )(place, own, other)


HALVES = ((0, 512), (512, 768))


def project_kernel(count, place_ref, x_hbm, mix_ref, far_mix_ref, *refs):
    pieces = refs[:count]
    own_ref, other_ref, x_ref, w_ref, x_sem, w_sem = refs[count:]
    chip_x, chip_y, level, core = (place_ref[i] for i in range(4))
    rows = own_ref.shape[0]
    x_copy = pltpu.make_async_copy(x_hbm, x_ref, x_sem)
    w_copies = [[] for _ in HALVES]
    for i, piece in enumerate(pieces):
        second, pair = GROUPS[i]
        for j, first in enumerate(FIRST[pair]):
            by_x = jnp.where(core == 0, first, second)
            by_y = jnp.where(core == 0, second, first)
            from_x = lax.rem(chip_x + by_x + RING, RING)
            from_y = lax.rem(chip_y + by_y + RING, RING)
            by = from_y * SIZES[4] + lax.div(from_x, 2)
            from_z = lax.rem(level + jnp.where(core == 0, SIZES[1] - by, by), SIZES[1])
            shard = lax.rem(from_x, 2) * SIZES[1] + from_z
            for h, (start, size) in enumerate(HALVES):
                columns = pl.ds(start, size)
                w_copies[h].append(
                    pltpu.make_async_copy(
                        piece.at[j, :, columns], w_ref.at[shard, :, columns], w_sem.at[h]
                    )
                )
    for copy in w_copies[0]:
        copy.start()
    x_copy.start()
    for copy in w_copies[1]:
        copy.start()
    mixes = (jnp.transpose(mix_ref[...]), jnp.transpose(far_mix_ref[...]))
    x_copy.wait()
    for copy in w_copies[0]:
        copy.wait()

    def product(column):
        w = w_ref[:, :, column : column + WIDTH].reshape(x_ref.shape[1], WIDTH)
        block = jnp.dot(x_ref[...], w, preferred_element_type=jnp.float32)
        return block[:rows], block[rows:]

    outs = (own_ref, other_ref)
    for out, block in zip(outs, product(0)):
        out[:, :WIDTH] = block
    for head in range(HEADS):
        for half in range(EXPERTS // 2):
            if head == 0 and half == 1:
                for copy in w_copies[1]:
                    copy.wait()
            expert = head * EXPERTS + 2 * half
            lanes = slice(WIDTH + head * DH, WIDTH + (head + 1) * DH)
            for out, mix, block in zip(outs, mixes, product(WIDTH + expert * DH)):
                part = (
                    mix[:, expert : expert + 1] * block[:, :DH]
                    + mix[:, expert + 1 : expert + 2] * block[:, DH:]
                )
                out[:, lanes] = part if half == 0 else out[:, lanes] + part


def project(place, x, mix, far_mix, pieces):
    rows = x.shape[0] // 2
    depth = x.shape[1]
    _, shard, columns = pieces[0].shape
    any_space = pl.BlockSpec(memory_space=pl.ANY)
    vmem = pl.BlockSpec(memory_space=pltpu.VMEM)
    count = len(pieces)
    return pl.pallas_call(
        functools.partial(project_kernel, count),
        in_specs=[pl.BlockSpec(memory_space=pltpu.SMEM), any_space, vmem, vmem]
        + [any_space] * count,
        out_specs=[vmem, vmem],
        out_shape=[jax.ShapeDtypeStruct((rows, 2 * WIDTH), jnp.float32)] * 2,
        scratch_shapes=[
            pltpu.VMEM(x.shape, x.dtype),
            pltpu.VMEM((2 * count, shard, columns), jnp.bfloat16),
            pltpu.SemaphoreType.DMA,
            pltpu.SemaphoreType.DMA((len(HALVES),)),
        ],
        compiler_params=VM,
        cost_estimate=pl.CostEstimate(
            flops=4 * rows * depth * columns,
            bytes_accessed=2 * depth * (2 * rows + columns),
            transcendentals=0,
        ),
    )(place, x, mix, far_mix, *pieces)


def query_kernel(x_ref, w_ref, q_ref, acc_ref):
    n = pl.program_id(0)
    count = w_ref.shape[0]
    w = jnp.concatenate(
        [
            jnp.concatenate([w_ref[i, :DH], w_ref[i, DH:]], axis=1)
            for i in range(count)
        ],
        axis=0,
    )
    part = jnp.dot(x_ref[...], w, preferred_element_type=jnp.float32)

    @pl.when(n == 0)
    def _():
        acc_ref[...] = part

    @pl.when(n > 0)
    def _():
        acc_ref[...] += part

    @pl.when(n == pl.num_programs(0) - 1)
    def _():
        q_ref[...] = acc_ref[...].astype(jnp.bfloat16)


def query(x, panels):
    rows, depth = x.shape
    shards = panels.shape[0] * panels.shape[1]
    steps = 4
    return pl.pallas_call(
        query_kernel,
        grid=(steps,),
        in_specs=[
            pl.BlockSpec((rows, depth // steps), lambda n: (0, n)),
            pl.BlockSpec((shards // steps, None, WIDTH, DH), lambda n: (n % 2, n // 2, 4, 0)),
        ],
        out_specs=pl.BlockSpec((rows, WIDTH), lambda n: (0, 0)),
        out_shape=jax.ShapeDtypeStruct((rows, WIDTH), jnp.bfloat16),
        scratch_shapes=[pltpu.VMEM((rows, WIDTH), jnp.float32)],
        compiler_params=VM,
        cost_estimate=pl.CostEstimate(
            flops=2 * rows * depth * WIDTH,
            bytes_accessed=2 * (rows * depth + depth * WIDTH),
            transcendentals=0,
        ),
    )(x, panels)


LOG2E = 1.4426950408889634
PANELS = 4


def attend_block(q_ref, kv, m_ref, l_ref, acc_ref, diagonal):
    scale = LOG2E / math.sqrt(DH)
    for head in range(HEADS):
        lanes = slice(head * DH, (head + 1) * DH)
        one = slice(head, head + 1)
        scores = lax.dot_general(
            kv[:, lanes],
            q_ref[:, lanes],
            (((1,), (1,)), ((), ())),
            preferred_element_type=jnp.float32,
        )
        values = kv[:, WIDTH + head * DH : WIDTH + (head + 1) * DH]
        if diagonal:
            k_pos = lax.broadcasted_iota(jnp.int32, scores.shape, 0)
            q_pos = lax.broadcasted_iota(jnp.int32, scores.shape, 1)
            scores = jnp.where(q_pos >= k_pos, scores, -jnp.inf)
            top = jnp.max(scores, axis=0, keepdims=True)
        else:
            before = m_ref[one]
            top = jnp.maximum(before, jnp.max(scores, axis=0, keepdims=True))
            rescale = jnp.exp2((before - top) * scale)
        weights = jnp.exp2((scores - top) * scale)
        total = jnp.sum(weights, axis=0, keepdims=True)
        update = lax.dot_general(
            values,
            weights.astype(jnp.bfloat16),
            (((0,), (0,)), ((), ())),
            preferred_element_type=jnp.float32,
        )
        m_ref[one] = top
        if diagonal:
            l_ref[one] = total
            acc_ref[lanes] = update
        else:
            l_ref[one] = l_ref[one] * rescale + total
            acc_ref[lanes] = acc_ref[lanes] * rescale + update


def attend_blocks(place_ref, needs, diagonal, q_ref, kv_refs, *state):
    row, side = place_ref[1], lax.div(place_ref[0], 2)
    for k, kv in enumerate(kv_refs):
        if diagonal and k == 0:
            attend_block(q_ref, kv, *state, True)
        else:
            pl.when((row >= needs[k][0]) & (side >= needs[k][1]))(
                functools.partial(attend_block, q_ref, kv, *state, False)
            )


def attend_early_kernel(needs, place_ref, q_ref, *refs):
    count = len(needs)
    attend_blocks(place_ref, needs, True, q_ref, refs[:count], *refs[count:])


def attend_late_kernel(needs, place_ref, q_ref, m_in, l_in, acc_in, mix_ref, panels, *refs):
    count = len(needs)
    out_hbm = refs[count]
    m_ref, l_ref, acc_ref, mixed_ref, w_ref, o_ref, w_sem, o_sem = refs[count + 1 :]
    depth = mixed_ref.shape[1]
    levels, lows = panels.shape[:2]
    w_copies = [
        pltpu.make_async_copy(
            panels.at[pl.ds(first, PANELS), low, pl.ds(0, depth)],
            w_ref.at[pl.ds(low * levels + first, PANELS)],
            w_sem,
        )
        for low in range(lows)
        for first in range(0, levels, PANELS)
    ]
    for copy in w_copies:
        copy.start()
    m_ref[...] = m_in[...]
    l_ref[...] = l_in[...]
    acc_ref[...] = acc_in[...]
    attend_blocks(place_ref, needs, False, q_ref, refs[:count], m_ref, l_ref, acc_ref)
    mix = jnp.transpose(mix_ref[...])
    for head in range(HEADS):
        attended = acc_ref[head * DH : (head + 1) * DH] / l_ref[head : head + 1]
        attended = jnp.transpose(attended).astype(jnp.bfloat16).astype(jnp.float32)
        for expert in range(EXPERTS):
            index = head * EXPERTS + expert
            mixed_ref[:, index * DH : (index + 1) * DH] = (
                mix[:, index : index + 1] * attended
            ).astype(jnp.bfloat16)
    for copy in w_copies:
        copy.wait()
    o_copies = []
    width = 2 * DH
    for i in range(0, levels * lows, 2):
        panel = jnp.concatenate([w_ref[i], w_ref[i + 1]], axis=1)
        block = jnp.dot(mixed_ref[...], panel, preferred_element_type=jnp.float32)
        o_ref[:, i * DH : i * DH + width] = block.astype(jnp.bfloat16)
        if i % PANELS == PANELS - 2:
            lanes = pl.ds((i + 2 - PANELS) * DH, PANELS * DH)
            o_copies.append(
                pltpu.make_async_copy(o_ref.at[:, lanes], out_hbm.at[:, lanes], o_sem)
            )
            o_copies[-1].start()
    for copy in o_copies:
        copy.wait()


def state_shapes(rows):
    return [(HEADS, rows), (HEADS, rows), (WIDTH, rows)]


def attend_cost(rows, count, flops):
    return pl.CostEstimate(
        flops=4 * rows * rows * DH * HEADS * count + flops,
        bytes_accessed=2 * rows * WIDTH * 2 * count,
        transcendentals=rows * rows * HEADS * count,
    )


def attend_early(place, q, blocks, needs):
    rows = q.shape[0]
    vmem = pl.BlockSpec(memory_space=pltpu.VMEM)
    return pl.pallas_call(
        functools.partial(attend_early_kernel, needs),
        in_specs=[pl.BlockSpec(memory_space=pltpu.SMEM)] + [vmem] * (1 + len(blocks)),
        out_specs=[vmem] * 3,
        out_shape=[jax.ShapeDtypeStruct(s, jnp.float32) for s in state_shapes(rows)],
        compiler_params=VM,
        cost_estimate=attend_cost(rows, len(blocks), 0),
    )(place, q, *blocks)


def attend_late(place, q, state, mix, panels, blocks, needs):
    rows = q.shape[0]
    depth = HEADS * EXPERTS * DH
    levels, lows, _, width = panels.shape
    columns = levels * lows * width
    vmem = pl.BlockSpec(memory_space=pltpu.VMEM)
    any_space = pl.BlockSpec(memory_space=pl.ANY)
    return pl.pallas_call(
        functools.partial(attend_late_kernel, needs),
        in_specs=[pl.BlockSpec(memory_space=pltpu.SMEM)]
        + [vmem] * 5
        + [any_space]
        + [vmem] * len(blocks),
        out_specs=any_space,
        out_shape=jax.ShapeDtypeStruct((rows, columns), jnp.bfloat16),
        scratch_shapes=[pltpu.VMEM(s, jnp.float32) for s in state_shapes(rows)]
        + [
            pltpu.VMEM((rows, depth), jnp.bfloat16),
            pltpu.VMEM((levels * lows, depth, width), jnp.bfloat16),
            pltpu.VMEM((rows, columns), jnp.bfloat16),
            pltpu.SemaphoreType.DMA,
            pltpu.SemaphoreType.DMA,
        ],
        compiler_params=VM,
        cost_estimate=attend_cost(rows, len(blocks), 2 * rows * depth * columns),
    )(place, q, *state, mix, panels, *blocks)


def on_device(
    tokens, w_query, w_key, w_value, w_out, value_experts, value_gates, output_experts, output_gates
):
    x = tokens[0]
    y, x_hi = lax.axis_index("y"), lax.axis_index("x_hi")
    chip_x = 2 * x_hi + lax.axis_index("x_lo")
    place = jnp.stack([chip_x, y, lax.axis_index("z"), lax.axis_index("core")]).astype(jnp.int32)
    shard = w_key.shape[0]
    block = lifted(
        jnp.concatenate([w_key.reshape(shard, -1), w_value.reshape(shard, -1)], axis=1)
    )
    value_mix = expert_mix(value_experts[0], value_gates[0])
    output_mix = expert_mix(output_experts[0], output_gates[0])
    output_mix = output_mix.astype(jnp.bfloat16).astype(jnp.float32)
    panel = jnp.concatenate(
        [
            w_out.reshape(-1, w_out.shape[3]),
            jnp.transpose(w_query, (1, 0, 2)).reshape(-1, DH),
        ],
        axis=0,
    )
    across = lax.ppermute(panel, "x_lo", [(0, 1), (1, 0)])
    far_mix = swapped(value_mix)
    both = packed(place, x, swapped(x))
    block, across = lax.optimization_barrier((block, across))
    low = lax.axis_index("x_lo") == 0
    pair = jnp.stack([jnp.where(low, panel, across), jnp.where(low, across, panel)])
    panels = lax.all_gather(pair, ("z", "core"), axis=0, tiled=False)
    mine, theirs = project(place, both, value_mix, far_mix, gathered(block))
    own = (mine + swapped(theirs)).astype(jnp.bfloat16)
    q = query(x, panels)

    other = lax.ppermute(own, "x_hi", [(0, 1), (1, 0)])
    own_1 = lax.ppermute(own, "y", [(0, 1), (1, 2), (2, 3)])
    own_3 = lax.ppermute(own, "y", [(0, 3)])
    own_2 = lax.ppermute(own, "y", [(0, 2), (1, 3)])
    other_1 = lax.ppermute(other, "y", [(0, 1), (1, 2), (2, 3)])
    other_3 = lax.ppermute(other, "y", [(0, 3)])
    other_2 = lax.ppermute(own_2, "x_hi", [(0, 1), (1, 0)])
    state = attend_early(
        place, q, [own, other, own_1, own_2, own_3], ((0, 0), (0, 1), (1, 0), (2, 0), (3, 0))
    )
    result = attend_late(
        place,
        q,
        state,
        output_mix,
        panels,
        [other_1, other_2, other_3],
        ((1, 0), (2, 0), (3, 0)),
    )
    return result[None]


def solution(mesh):
    grid = Mesh(mesh.devices.reshape(SIZES), AXES)
    seq = P(FSDP, CTX, None, None)
    in_specs = (
        P(FSDP, CTX, None),
        P(FSDP, None, None),
        P(FSDP, None, None),
        P(FSDP, None, None, None),
        P(None, None, None, FSDP),
        seq,
        seq,
        seq,
        seq,
    )
    return jax.shard_map(
        on_device, mesh=grid, in_specs=in_specs, out_specs=P(FSDP, CTX, None), check_vma=False
    )
```

```python
import functools
import itertools
import math

import jax
import jax.numpy as jnp
from jax import lax
from jax.experimental import pallas as pl
from jax.experimental.pallas import tpu as pltpu
from jax.sharding import Mesh
from jax.sharding import PartitionSpec as P

AXES = ("x_lo", "z", "core", "y", "x_hi")
SIZES = (2, 8, 2, 4, 2)
FSDP = ("x_lo", "z", "core")
CTX = ("y", "x_hi")
HEADS, EXPERTS, DH = 2, 4, 128
WIDTH = HEADS * DH
MIB = 1 << 20


def expert_mix(indices, gates):
    one_hot = (indices[..., None] == jnp.arange(EXPERTS, dtype=jnp.int32)).astype(jnp.float32)
    mix = jnp.sum(gates.astype(jnp.float32)[..., None] * one_hot, axis=-2)
    return mix.reshape(mix.shape[0], HEADS * EXPERTS).T


RING = 4
VM = pltpu.CompilerParams(vmem_limit_bytes=32 * MIB)


def moved(x, target):
    pairs = []
    for source, (x_lo, z, core, y, x_hi) in enumerate(itertools.product(*map(range, SIZES))):
        to_x, to_y, to_core = target(2 * x_hi + x_lo, y, core)
        to_x, to_y = to_x % RING, to_y % RING
        place = (((to_x % 2) * SIZES[1] + z) * SIZES[2] + to_core) * SIZES[3] + to_y
        pairs.append((source, place * SIZES[4] + to_x // 2))
    return lax.ppermute(x, AXES, pairs)


def hop(x, by, phase):
    return moved(
        x, lambda cx, cy, core: (cx + by, cy, core) if core == phase else (cx, cy + by, core)
    )


def swapped(x):
    return lax.ppermute(x, "core", [(0, 1), (1, 0)])


FIRST = ((0, -1), (1, 2))
GROUPS = ((0, 0), (0, 1), (-1, 0), (1, 1), (1, 0), (-1, 1), (2, 0), (2, 1))


def lifted(x):
    pairs = []
    for source, (x_lo, z, core, y, x_hi) in enumerate(itertools.product(*map(range, SIZES))):
        by = y * SIZES[4] + x_hi
        to_z = (z + by if core == 0 else z - by) % SIZES[1]
        place = ((x_lo * SIZES[1] + to_z) * SIZES[2] + core) * SIZES[3] + y
        pairs.append((source, place * SIZES[4] + x_hi))
    return lax.ppermute(x, AXES, pairs)


def gathered(block):
    up = hop(block, 1, 0)
    down = hop(block, -1, 0)
    across = hop(block, 2, 0)
    near = jnp.stack([block, up])
    far = jnp.stack([down, across])
    near_up = hop(near, 1, 1)
    far_down = hop(far, -1, 1)
    near_down = hop(near, -1, 1)
    far_up = hop(far, 1, 1)
    near_across = hop(near_up, 1, 1)
    far_across = hop(far_down, -1, 1)
    return [near, far, near_up, far_down, near_down, far_up, near_across, far_across]


def pack_kernel(place_ref, own_ref, other_ref, out_ref):
    rows = own_ref.shape[0]
    core = place_ref[3]
    for i in range(SIZES[0] * SIZES[1]):
        lanes = pl.ds(pl.multiple_of((SIZES[2] * i + core) * DH, DH), DH)
        out_ref[:rows, i * DH : (i + 1) * DH] = own_ref[:, lanes]
        out_ref[rows:, i * DH : (i + 1) * DH] = other_ref[:, lanes]


def packed(place, own, other):
    rows, depth = own.shape
    vmem = pl.BlockSpec(memory_space=pltpu.VMEM)
    return pl.pallas_call(
        pack_kernel,
        in_specs=[pl.BlockSpec(memory_space=pltpu.SMEM), vmem, vmem],
        out_specs=vmem,
        out_shape=jax.ShapeDtypeStruct((2 * rows, depth // 2), own.dtype),
        compiler_params=VM,
        cost_estimate=pl.CostEstimate(
            flops=0, bytes_accessed=6 * rows * depth, transcendentals=0
        ),
    )(place, own, other)


HALVES = ((0, 512), (512, 768))


def project_kernel(count, place_ref, x_hbm, mix_ref, far_mix_ref, *refs):
    pieces = refs[:count]
    own_ref, other_ref, x_ref, w_ref, x_sem, w_sem = refs[count:]
    chip_x, chip_y, level, core = (place_ref[i] for i in range(4))
    rows = own_ref.shape[0]
    x_copy = pltpu.make_async_copy(x_hbm, x_ref, x_sem)
    w_copies = [[] for _ in HALVES]
    for i, piece in enumerate(pieces):
        second, pair = GROUPS[i]
        for j, first in enumerate(FIRST[pair]):
            by_x = jnp.where(core == 0, first, second)
            by_y = jnp.where(core == 0, second, first)
            from_x = lax.rem(chip_x + by_x + RING, RING)
            from_y = lax.rem(chip_y + by_y + RING, RING)
            by = from_y * SIZES[4] + lax.div(from_x, 2)
            from_z = lax.rem(level + jnp.where(core == 0, SIZES[1] - by, by), SIZES[1])
            shard = lax.rem(from_x, 2) * SIZES[1] + from_z
            for h, (start, size) in enumerate(HALVES):
                columns = pl.ds(start, size)
                w_copies[h].append(
                    pltpu.make_async_copy(
                        piece.at[j, :, columns], w_ref.at[shard, :, columns], w_sem.at[h]
                    )
                )
    for copy in w_copies[0]:
        copy.start()
    x_copy.start()
    for copy in w_copies[1]:
        copy.start()
    mixes = (jnp.transpose(mix_ref[...]), jnp.transpose(far_mix_ref[...]))
    x_copy.wait()
    for copy in w_copies[0]:
        copy.wait()

    def product(column):
        w = w_ref[:, :, column : column + WIDTH].reshape(x_ref.shape[1], WIDTH)
        block = jnp.dot(x_ref[...], w, preferred_element_type=jnp.float32)
        return block[:rows], block[rows:]

    outs = (own_ref, other_ref)
    for out, block in zip(outs, product(0)):
        out[:, :WIDTH] = block
    for head in range(HEADS):
        for half in range(EXPERTS // 2):
            if head == 0 and half == 1:
                for copy in w_copies[1]:
                    copy.wait()
            expert = head * EXPERTS + 2 * half
            lanes = slice(WIDTH + head * DH, WIDTH + (head + 1) * DH)
            for out, mix, block in zip(outs, mixes, product(WIDTH + expert * DH)):
                part = (
                    mix[:, expert : expert + 1] * block[:, :DH]
                    + mix[:, expert + 1 : expert + 2] * block[:, DH:]
                )
                out[:, lanes] = part if half == 0 else out[:, lanes] + part


def project(place, x, mix, far_mix, pieces):
    rows = x.shape[0] // 2
    depth = x.shape[1]
    _, shard, columns = pieces[0].shape
    any_space = pl.BlockSpec(memory_space=pl.ANY)
    vmem = pl.BlockSpec(memory_space=pltpu.VMEM)
    count = len(pieces)
    return pl.pallas_call(
        functools.partial(project_kernel, count),
        in_specs=[pl.BlockSpec(memory_space=pltpu.SMEM), any_space, vmem, vmem]
        + [any_space] * count,
        out_specs=[vmem, vmem],
        out_shape=[jax.ShapeDtypeStruct((rows, 2 * WIDTH), jnp.float32)] * 2,
        scratch_shapes=[
            pltpu.VMEM(x.shape, x.dtype),
            pltpu.VMEM((2 * count, shard, columns), jnp.bfloat16),
            pltpu.SemaphoreType.DMA,
            pltpu.SemaphoreType.DMA((len(HALVES),)),
        ],
        compiler_params=VM,
        cost_estimate=pl.CostEstimate(
            flops=4 * rows * depth * columns,
            bytes_accessed=2 * depth * (2 * rows + columns),
            transcendentals=0,
        ),
    )(place, x, mix, far_mix, *pieces)


def query_kernel(x_ref, w_ref, q_ref, acc_ref):
    n = pl.program_id(0)
    count = w_ref.shape[0]
    w = jnp.concatenate(
        [
            jnp.concatenate([w_ref[i, :DH], w_ref[i, DH:]], axis=1)
            for i in range(count)
        ],
        axis=0,
    )
    part = jnp.dot(x_ref[...], w, preferred_element_type=jnp.float32)

    @pl.when(n == 0)
    def _():
        acc_ref[...] = part

    @pl.when(n > 0)
    def _():
        acc_ref[...] += part

    @pl.when(n == pl.num_programs(0) - 1)
    def _():
        q_ref[...] = acc_ref[...].astype(jnp.bfloat16)


def query(x, panels):
    rows, depth = x.shape
    shards = panels.shape[0] * panels.shape[1]
    steps = 4
    return pl.pallas_call(
        query_kernel,
        grid=(steps,),
        in_specs=[
            pl.BlockSpec((rows, depth // steps), lambda n: (0, n)),
            pl.BlockSpec((shards // steps, None, WIDTH, DH), lambda n: (n % 2, n // 2, 4, 0)),
        ],
        out_specs=pl.BlockSpec((rows, WIDTH), lambda n: (0, 0)),
        out_shape=jax.ShapeDtypeStruct((rows, WIDTH), jnp.bfloat16),
        scratch_shapes=[pltpu.VMEM((rows, WIDTH), jnp.float32)],
        compiler_params=VM,
        cost_estimate=pl.CostEstimate(
            flops=2 * rows * depth * WIDTH,
            bytes_accessed=2 * (rows * depth + depth * WIDTH),
            transcendentals=0,
        ),
    )(x, panels)


LOG2E = 1.4426950408889634
PANELS = 4


def attend_block(q_ref, kv, m_ref, l_ref, acc_ref, diagonal):
    scale = LOG2E / math.sqrt(DH)
    for head in range(HEADS):
        lanes = slice(head * DH, (head + 1) * DH)
        one = slice(head, head + 1)
        scores = lax.dot_general(
            kv[:, lanes],
            q_ref[:, lanes],
            (((1,), (1,)), ((), ())),
            preferred_element_type=jnp.float32,
        )
        values = kv[:, WIDTH + head * DH : WIDTH + (head + 1) * DH]
        if diagonal:
            k_pos = lax.broadcasted_iota(jnp.int32, scores.shape, 0)
            q_pos = lax.broadcasted_iota(jnp.int32, scores.shape, 1)
            scores = jnp.where(q_pos >= k_pos, scores, -jnp.inf)
            top = jnp.max(scores, axis=0, keepdims=True)
        else:
            before = m_ref[one]
            top = jnp.maximum(before, jnp.max(scores, axis=0, keepdims=True))
            rescale = jnp.exp2((before - top) * scale)
        weights = jnp.exp2((scores - top) * scale)
        total = jnp.sum(weights, axis=0, keepdims=True)
        update = lax.dot_general(
            values,
            weights.astype(jnp.bfloat16),
            (((0,), (0,)), ((), ())),
            preferred_element_type=jnp.float32,
        )
        m_ref[one] = top
        if diagonal:
            l_ref[one] = total
            acc_ref[lanes] = update
        else:
            l_ref[one] = l_ref[one] * rescale + total
            acc_ref[lanes] = acc_ref[lanes] * rescale + update


def attend_blocks(place_ref, needs, diagonal, q_ref, kv_refs, *state):
    row, side = place_ref[1], lax.div(place_ref[0], 2)
    for k, kv in enumerate(kv_refs):
        if diagonal and k == 0:
            attend_block(q_ref, kv, *state, True)
        else:
            pl.when((row >= needs[k][0]) & (side >= needs[k][1]))(
                functools.partial(attend_block, q_ref, kv, *state, False)
            )


def attend_early_kernel(needs, place_ref, q_ref, *refs):
    count = len(needs)
    attend_blocks(place_ref, needs, True, q_ref, refs[:count], *refs[count:])


def attend_late_kernel(needs, place_ref, q_ref, m_in, l_in, acc_in, mix_ref, panels, *refs):
    count = len(needs)
    out_hbm = refs[count]
    m_ref, l_ref, acc_ref, mixed_ref, w_ref, o_ref, w_sem, o_sem = refs[count + 1 :]
    depth = mixed_ref.shape[1]
    levels, lows = panels.shape[:2]
    w_copies = [
        pltpu.make_async_copy(
            panels.at[pl.ds(first, PANELS), low, pl.ds(0, depth)],
            w_ref.at[pl.ds(low * levels + first, PANELS)],
            w_sem,
        )
        for low in range(lows)
        for first in range(0, levels, PANELS)
    ]
    for copy in w_copies:
        copy.start()
    m_ref[...] = m_in[...]
    l_ref[...] = l_in[...]
    acc_ref[...] = acc_in[...]
    attend_blocks(place_ref, needs, False, q_ref, refs[:count], m_ref, l_ref, acc_ref)
    mix = jnp.transpose(mix_ref[...])
    for head in range(HEADS):
        attended = acc_ref[head * DH : (head + 1) * DH] / l_ref[head : head + 1]
        attended = jnp.transpose(attended).astype(jnp.bfloat16).astype(jnp.float32)
        for expert in range(EXPERTS):
            index = head * EXPERTS + expert
            mixed_ref[:, index * DH : (index + 1) * DH] = (
                mix[:, index : index + 1] * attended
            ).astype(jnp.bfloat16)
    for copy in w_copies:
        copy.wait()
    o_copies = []
    width = 2 * DH
    for i in range(0, levels * lows, 2):
        panel = jnp.concatenate([w_ref[i], w_ref[i + 1]], axis=1)
        block = jnp.dot(mixed_ref[...], panel, preferred_element_type=jnp.float32)
        o_ref[:, i * DH : i * DH + width] = block.astype(jnp.bfloat16)
        if i % PANELS == PANELS - 2:
            lanes = pl.ds((i + 2 - PANELS) * DH, PANELS * DH)
            o_copies.append(
                pltpu.make_async_copy(o_ref.at[:, lanes], out_hbm.at[:, lanes], o_sem)
            )
            o_copies[-1].start()
    for copy in o_copies:
        copy.wait()


def state_shapes(rows):
    return [(HEADS, rows), (HEADS, rows), (WIDTH, rows)]


def attend_cost(rows, count, flops):
    return pl.CostEstimate(
        flops=4 * rows * rows * DH * HEADS * count + flops,
        bytes_accessed=2 * rows * WIDTH * 2 * count,
        transcendentals=rows * rows * HEADS * count,
    )


def attend_early(place, q, blocks, needs):
    rows = q.shape[0]
    vmem = pl.BlockSpec(memory_space=pltpu.VMEM)
    return pl.pallas_call(
        functools.partial(attend_early_kernel, needs),
        in_specs=[pl.BlockSpec(memory_space=pltpu.SMEM)] + [vmem] * (1 + len(blocks)),
        out_specs=[vmem] * 3,
        out_shape=[jax.ShapeDtypeStruct(s, jnp.float32) for s in state_shapes(rows)],
        compiler_params=VM,
        cost_estimate=attend_cost(rows, len(blocks), 0),
    )(place, q, *blocks)


def attend_late(place, q, state, mix, panels, blocks, needs):
    rows = q.shape[0]
    depth = HEADS * EXPERTS * DH
    levels, lows, _, width = panels.shape
    columns = levels * lows * width
    vmem = pl.BlockSpec(memory_space=pltpu.VMEM)
    any_space = pl.BlockSpec(memory_space=pl.ANY)
    return pl.pallas_call(
        functools.partial(attend_late_kernel, needs),
        in_specs=[pl.BlockSpec(memory_space=pltpu.SMEM)]
        + [vmem] * 5
        + [any_space]
        + [vmem] * len(blocks),
        out_specs=any_space,
        out_shape=jax.ShapeDtypeStruct((rows, columns), jnp.bfloat16),
        scratch_shapes=[pltpu.VMEM(s, jnp.float32) for s in state_shapes(rows)]
        + [
            pltpu.VMEM((rows, depth), jnp.bfloat16),
            pltpu.VMEM((levels * lows, depth, width), jnp.bfloat16),
            pltpu.VMEM((rows, columns), jnp.bfloat16),
            pltpu.SemaphoreType.DMA,
            pltpu.SemaphoreType.DMA,
        ],
        compiler_params=VM,
        cost_estimate=attend_cost(rows, len(blocks), 2 * rows * depth * columns),
    )(place, q, *state, mix, panels, *blocks)


def on_device(
    tokens, w_query, w_key, w_value, w_out, value_experts, value_gates, output_experts, output_gates
):
    x = tokens[0]
    y, x_hi = lax.axis_index("y"), lax.axis_index("x_hi")
    chip_x = 2 * x_hi + lax.axis_index("x_lo")
    place = jnp.stack([chip_x, y, lax.axis_index("z"), lax.axis_index("core")]).astype(jnp.int32)
    shard = w_key.shape[0]
    block = lifted(
        jnp.concatenate([w_key.reshape(shard, -1), w_value.reshape(shard, -1)], axis=1)
    )
    value_mix = expert_mix(value_experts[0], value_gates[0])
    output_mix = expert_mix(output_experts[0], output_gates[0])
    output_mix = output_mix.astype(jnp.bfloat16).astype(jnp.float32)
    panel = jnp.concatenate(
        [
            w_out.reshape(-1, w_out.shape[3]),
            jnp.transpose(w_query, (1, 0, 2)).reshape(-1, DH),
        ],
        axis=0,
    )
    across = lax.ppermute(panel, "x_lo", [(0, 1), (1, 0)])
    far_mix = swapped(value_mix)
    both = packed(place, x, swapped(x))
    block, across = lax.optimization_barrier((block, across))
    low = lax.axis_index("x_lo") == 0
    pair = jnp.stack([jnp.where(low, panel, across), jnp.where(low, across, panel)])
    panels = lax.all_gather(pair, ("z", "core"), axis=0, tiled=False)
    mine, theirs = project(place, both, value_mix, far_mix, gathered(block))
    own = (mine + swapped(theirs)).astype(jnp.bfloat16)
    q = query(x, panels)

    other = lax.ppermute(own, "x_hi", [(0, 1), (1, 0)])
    own_1 = lax.ppermute(own, "y", [(0, 1), (1, 2), (2, 3)])
    own_3 = lax.ppermute(own, "y", [(0, 3)])
    own_2 = lax.ppermute(own, "y", [(0, 2), (1, 3)])
    other_1 = lax.ppermute(other, "y", [(0, 1), (1, 2), (2, 3)])
    other_3 = lax.ppermute(other, "y", [(0, 3)])
    other_2 = lax.ppermute(own_2, "x_hi", [(0, 1), (1, 0)])
    state = attend_early(
        place, q, [own, other, own_1, own_2, own_3], ((0, 0), (0, 1), (1, 0), (2, 0), (3, 0))
    )
    result = attend_late(
        place,
        q,
        state,
        output_mix,
        panels,
        [other_1, other_2, other_3],
        ((1, 0), (2, 0), (3, 0)),
    )
    return result[None]


def solution(mesh):
    grid = Mesh(mesh.devices.reshape(SIZES), AXES)
    seq = P(FSDP, CTX, None, None)
    in_specs = (
        P(FSDP, CTX, None),
        P(FSDP, None, None),
        P(FSDP, None, None),
        P(FSDP, None, None, None),
        P(None, None, None, FSDP),
        seq,
        seq,
        seq,
        seq,
    )
    return jax.shard_map(
        on_device, mesh=grid, in_specs=in_specs, out_specs=P(FSDP, CTX, None), check_vma=False
    )
```

```python
import functools
import itertools
import math

import jax
import jax.numpy as jnp
from jax import lax
from jax.experimental import pallas as pl
from jax.experimental.pallas import tpu as pltpu
from jax.sharding import Mesh
from jax.sharding import PartitionSpec as P

AXES = ("x_lo", "z", "core", "y", "x_hi")
SIZES = (2, 8, 2, 4, 2)
FSDP = ("x_lo", "z", "core")
CTX = ("y", "x_hi")
HEADS, EXPERTS, DH = 2, 4, 128
WIDTH = HEADS * DH
MIB = 1 << 20


def expert_mix(indices, gates):
    one_hot = (indices[..., None] == jnp.arange(EXPERTS, dtype=jnp.int32)).astype(jnp.float32)
    mix = jnp.sum(gates.astype(jnp.float32)[..., None] * one_hot, axis=-2)
    return mix.reshape(mix.shape[0], HEADS * EXPERTS).T


RING = 4
VM = pltpu.CompilerParams(vmem_limit_bytes=32 * MIB)


def moved(x, target):
    pairs = []
    for source, (x_lo, z, core, y, x_hi) in enumerate(itertools.product(*map(range, SIZES))):
        to_x, to_y, to_core = target(2 * x_hi + x_lo, y, core)
        to_x, to_y = to_x % RING, to_y % RING
        place = (((to_x % 2) * SIZES[1] + z) * SIZES[2] + to_core) * SIZES[3] + to_y
        pairs.append((source, place * SIZES[4] + to_x // 2))
    return lax.ppermute(x, AXES, pairs)


def hop(x, by, phase):
    return moved(
        x, lambda cx, cy, core: (cx + by, cy, core) if core == phase else (cx, cy + by, core)
    )


def swapped(x):
    return lax.ppermute(x, "core", [(0, 1), (1, 0)])


FIRST = ((0, -1), (1, 2))
GROUPS = ((0, 0), (0, 1), (-1, 0), (1, 1), (1, 0), (-1, 1), (2, 0), (2, 1))


def lifted(x):
    pairs = []
    for source, (x_lo, z, core, y, x_hi) in enumerate(itertools.product(*map(range, SIZES))):
        by = y * SIZES[4] + x_hi
        to_z = (z + by if core == 0 else z - by) % SIZES[1]
        place = ((x_lo * SIZES[1] + to_z) * SIZES[2] + core) * SIZES[3] + y
        pairs.append((source, place * SIZES[4] + x_hi))
    return lax.ppermute(x, AXES, pairs)


def gathered(block):
    up = hop(block, 1, 0)
    down = hop(block, -1, 0)
    across = hop(block, 2, 0)
    near = jnp.stack([block, up])
    far = jnp.stack([down, across])
    near_up = hop(near, 1, 1)
    far_down = hop(far, -1, 1)
    near_down = hop(near, -1, 1)
    far_up = hop(far, 1, 1)
    near_across = hop(near_up, 1, 1)
    far_across = hop(far_down, -1, 1)
    return [near, far, near_up, far_down, near_down, far_up, near_across, far_across]


def pack_kernel(place_ref, own_ref, other_ref, out_ref):
    rows = own_ref.shape[0]
    chip_x, chip_y, level, core = (place_ref[i] for i in range(4))
    for i, (second, pair) in enumerate(GROUPS):
        for j, first in enumerate(FIRST[pair]):
            by_x = jnp.where(core == 0, first, second)
            by_y = jnp.where(core == 0, second, first)
            from_x = lax.rem(chip_x + by_x + RING, RING)
            from_y = lax.rem(chip_y + by_y + RING, RING)
            by = from_y * SIZES[4] + lax.div(from_x, 2)
            from_z = lax.rem(level + jnp.where(core == 0, SIZES[1] - by, by), SIZES[1])
            shard = (lax.rem(from_x, 2) * SIZES[1] + from_z) * SIZES[2] + core
            lanes = pl.ds(pl.multiple_of(shard * DH, DH), DH)
            to = slice((2 * i + j) * DH, (2 * i + j + 1) * DH)
            out_ref[:rows, to] = own_ref[:, lanes]
            out_ref[rows:, to] = other_ref[:, lanes]


def packed(place, own, other):
    rows, depth = own.shape
    vmem = pl.BlockSpec(memory_space=pltpu.VMEM)
    return pl.pallas_call(
        pack_kernel,
        in_specs=[pl.BlockSpec(memory_space=pltpu.SMEM), vmem, vmem],
        out_specs=vmem,
        out_shape=jax.ShapeDtypeStruct((2 * rows, depth // 2), own.dtype),
        compiler_params=VM,
        cost_estimate=pl.CostEstimate(
            flops=0, bytes_accessed=6 * rows * depth, transcendentals=0
        ),
    )(place, own, other)


def project_kernel(count, place_ref, x_ref, mix_ref, far_mix_ref, *refs):
    pieces = refs[:count]
    outs = refs[count:]
    rows = outs[0].shape[0]
    mixes = (jnp.transpose(mix_ref[...]), jnp.transpose(far_mix_ref[...]))

    def product(column):
        w = jnp.concatenate(
            [piece[j, :, column : column + WIDTH] for piece in pieces for j in range(2)], axis=0
        )
        block = jnp.dot(x_ref[...], w, preferred_element_type=jnp.float32)
        return block[:rows], block[rows:]

    for out, block in zip(outs, product(0)):
        out[:, :WIDTH] = block
    for head in range(HEADS):
        for half in range(EXPERTS // 2):
            expert = head * EXPERTS + 2 * half
            lanes = slice(WIDTH + head * DH, WIDTH + (head + 1) * DH)
            for out, mix, block in zip(outs, mixes, product(WIDTH + expert * DH)):
                part = (
                    mix[:, expert : expert + 1] * block[:, :DH]
                    + mix[:, expert + 1 : expert + 2] * block[:, DH:]
                )
                out[:, lanes] = part if half == 0 else out[:, lanes] + part


def project(place, x, mix, far_mix, pieces):
    rows = x.shape[0] // 2
    depth = x.shape[1]
    _, shard, columns = pieces[0].shape
    vmem = pl.BlockSpec(memory_space=pltpu.VMEM)
    count = len(pieces)
    return pl.pallas_call(
        functools.partial(project_kernel, count),
        in_specs=[pl.BlockSpec(memory_space=pltpu.SMEM)] + [vmem] * (3 + count),
        out_specs=[vmem, vmem],
        out_shape=[jax.ShapeDtypeStruct((rows, 2 * WIDTH), jnp.float32)] * 2,
        compiler_params=VM,
        cost_estimate=pl.CostEstimate(
            flops=4 * rows * depth * columns,
            bytes_accessed=2 * depth * (2 * rows + columns),
            transcendentals=0,
        ),
    )(place, x, mix, far_mix, *pieces)


def query_kernel(x_ref, w_ref, q_ref, acc_ref):
    n = pl.program_id(0)
    count = w_ref.shape[0]
    w = jnp.concatenate(
        [
            jnp.concatenate([w_ref[i, :DH], w_ref[i, DH:]], axis=1)
            for i in range(count)
        ],
        axis=0,
    )
    part = jnp.dot(x_ref[...], w, preferred_element_type=jnp.float32)

    @pl.when(n == 0)
    def _():
        acc_ref[...] = part

    @pl.when(n > 0)
    def _():
        acc_ref[...] += part

    @pl.when(n == pl.num_programs(0) - 1)
    def _():
        q_ref[...] = acc_ref[...].astype(jnp.bfloat16)


def query(x, panels):
    rows, depth = x.shape
    shards = panels.shape[0] * panels.shape[1]
    steps = 4
    return pl.pallas_call(
        query_kernel,
        grid=(steps,),
        in_specs=[
            pl.BlockSpec((rows, depth // steps), lambda n: (0, n)),
            pl.BlockSpec((shards // steps, None, WIDTH, DH), lambda n: (n % 2, n // 2, 4, 0)),
        ],
        out_specs=pl.BlockSpec((rows, WIDTH), lambda n: (0, 0)),
        out_shape=jax.ShapeDtypeStruct((rows, WIDTH), jnp.bfloat16),
        scratch_shapes=[pltpu.VMEM((rows, WIDTH), jnp.float32)],
        compiler_params=VM,
        cost_estimate=pl.CostEstimate(
            flops=2 * rows * depth * WIDTH,
            bytes_accessed=2 * (rows * depth + depth * WIDTH),
            transcendentals=0,
        ),
    )(x, panels)


LOG2E = 1.4426950408889634
PANELS = 4


def attend_block(q_ref, kv, m_ref, l_ref, acc_ref, diagonal):
    scale = LOG2E / math.sqrt(DH)
    for head in range(HEADS):
        lanes = slice(head * DH, (head + 1) * DH)
        one = slice(head, head + 1)
        scores = lax.dot_general(
            kv[:, lanes],
            q_ref[:, lanes],
            (((1,), (1,)), ((), ())),
            preferred_element_type=jnp.float32,
        )
        values = kv[:, WIDTH + head * DH : WIDTH + (head + 1) * DH]
        if diagonal:
            k_pos = lax.broadcasted_iota(jnp.int32, scores.shape, 0)
            q_pos = lax.broadcasted_iota(jnp.int32, scores.shape, 1)
            scores = jnp.where(q_pos >= k_pos, scores, -jnp.inf)
            top = jnp.max(scores, axis=0, keepdims=True)
        else:
            before = m_ref[one]
            top = jnp.maximum(before, jnp.max(scores, axis=0, keepdims=True))
            rescale = jnp.exp2((before - top) * scale)
        weights = jnp.exp2((scores - top) * scale)
        total = jnp.sum(weights, axis=0, keepdims=True)
        update = lax.dot_general(
            values,
            weights.astype(jnp.bfloat16),
            (((0,), (0,)), ((), ())),
            preferred_element_type=jnp.float32,
        )
        m_ref[one] = top
        if diagonal:
            l_ref[one] = total
            acc_ref[lanes] = update
        else:
            l_ref[one] = l_ref[one] * rescale + total
            acc_ref[lanes] = acc_ref[lanes] * rescale + update


def attend_blocks(place_ref, needs, diagonal, q_ref, kv_refs, *state):
    row, side = place_ref[1], lax.div(place_ref[0], 2)
    for k, kv in enumerate(kv_refs):
        if diagonal and k == 0:
            attend_block(q_ref, kv, *state, True)
        else:
            pl.when((row >= needs[k][0]) & (side >= needs[k][1]))(
                functools.partial(attend_block, q_ref, kv, *state, False)
            )


def attend_early_kernel(needs, place_ref, q_ref, *refs):
    count = len(needs)
    attend_blocks(place_ref, needs, True, q_ref, refs[:count], *refs[count:])


def attend_late_kernel(needs, place_ref, q_ref, m_in, l_in, acc_in, mix_ref, panels, *refs):
    count = len(needs)
    out_hbm = refs[count]
    m_ref, l_ref, acc_ref, mixed_ref, w_ref, o_ref, w_sem, o_sem = refs[count + 1 :]
    depth = mixed_ref.shape[1]
    levels, lows = panels.shape[:2]
    w_copies = [
        pltpu.make_async_copy(
            panels.at[pl.ds(first, PANELS), low, pl.ds(0, depth)],
            w_ref.at[pl.ds(low * levels + first, PANELS)],
            w_sem,
        )
        for low in range(lows)
        for first in range(0, levels, PANELS)
    ]
    for copy in w_copies:
        copy.start()
    m_ref[...] = m_in[...]
    l_ref[...] = l_in[...]
    acc_ref[...] = acc_in[...]
    attend_blocks(place_ref, needs, False, q_ref, refs[:count], m_ref, l_ref, acc_ref)
    mix = jnp.transpose(mix_ref[...])
    for head in range(HEADS):
        attended = acc_ref[head * DH : (head + 1) * DH] / l_ref[head : head + 1]
        attended = jnp.transpose(attended).astype(jnp.bfloat16).astype(jnp.float32)
        for expert in range(EXPERTS):
            index = head * EXPERTS + expert
            mixed_ref[:, index * DH : (index + 1) * DH] = (
                mix[:, index : index + 1] * attended
            ).astype(jnp.bfloat16)
    for copy in w_copies:
        copy.wait()
    o_copies = []
    width = 2 * DH
    for i in range(0, levels * lows, 2):
        panel = jnp.concatenate([w_ref[i], w_ref[i + 1]], axis=1)
        block = jnp.dot(mixed_ref[...], panel, preferred_element_type=jnp.float32)
        o_ref[:, i * DH : i * DH + width] = block.astype(jnp.bfloat16)
        if i % PANELS == PANELS - 2:
            lanes = pl.ds((i + 2 - PANELS) * DH, PANELS * DH)
            o_copies.append(
                pltpu.make_async_copy(o_ref.at[:, lanes], out_hbm.at[:, lanes], o_sem)
            )
            o_copies[-1].start()
    for copy in o_copies:
        copy.wait()


def state_shapes(rows):
    return [(HEADS, rows), (HEADS, rows), (WIDTH, rows)]


def attend_cost(rows, count, flops):
    return pl.CostEstimate(
        flops=4 * rows * rows * DH * HEADS * count + flops,
        bytes_accessed=2 * rows * WIDTH * 2 * count,
        transcendentals=rows * rows * HEADS * count,
    )


def attend_early(place, q, blocks, needs):
    rows = q.shape[0]
    vmem = pl.BlockSpec(memory_space=pltpu.VMEM)
    return pl.pallas_call(
        functools.partial(attend_early_kernel, needs),
        in_specs=[pl.BlockSpec(memory_space=pltpu.SMEM)] + [vmem] * (1 + len(blocks)),
        out_specs=[vmem] * 3,
        out_shape=[jax.ShapeDtypeStruct(s, jnp.float32) for s in state_shapes(rows)],
        compiler_params=VM,
        cost_estimate=attend_cost(rows, len(blocks), 0),
    )(place, q, *blocks)


def attend_late(place, q, state, mix, panels, blocks, needs):
    rows = q.shape[0]
    depth = HEADS * EXPERTS * DH
    levels, lows, _, width = panels.shape
    columns = levels * lows * width
    vmem = pl.BlockSpec(memory_space=pltpu.VMEM)
    any_space = pl.BlockSpec(memory_space=pl.ANY)
    return pl.pallas_call(
        functools.partial(attend_late_kernel, needs),
        in_specs=[pl.BlockSpec(memory_space=pltpu.SMEM)]
        + [vmem] * 5
        + [any_space]
        + [vmem] * len(blocks),
        out_specs=any_space,
        out_shape=jax.ShapeDtypeStruct((rows, columns), jnp.bfloat16),
        scratch_shapes=[pltpu.VMEM(s, jnp.float32) for s in state_shapes(rows)]
        + [
            pltpu.VMEM((rows, depth), jnp.bfloat16),
            pltpu.VMEM((levels * lows, depth, width), jnp.bfloat16),
            pltpu.VMEM((rows, columns), jnp.bfloat16),
            pltpu.SemaphoreType.DMA,
            pltpu.SemaphoreType.DMA,
        ],
        compiler_params=VM,
        cost_estimate=attend_cost(rows, len(blocks), 2 * rows * depth * columns),
    )(place, q, *state, mix, panels, *blocks)


def on_device(
    tokens, w_query, w_key, w_value, w_out, value_experts, value_gates, output_experts, output_gates
):
    x = tokens[0]
    y, x_hi = lax.axis_index("y"), lax.axis_index("x_hi")
    chip_x = 2 * x_hi + lax.axis_index("x_lo")
    place = jnp.stack([chip_x, y, lax.axis_index("z"), lax.axis_index("core")]).astype(jnp.int32)
    shard = w_key.shape[0]
    block = lifted(
        jnp.concatenate([w_key.reshape(shard, -1), w_value.reshape(shard, -1)], axis=1)
    )
    value_mix = expert_mix(value_experts[0], value_gates[0])
    output_mix = expert_mix(output_experts[0], output_gates[0])
    output_mix = output_mix.astype(jnp.bfloat16).astype(jnp.float32)
    panel = jnp.concatenate(
        [
            w_out.reshape(-1, w_out.shape[3]),
            jnp.transpose(w_query, (1, 0, 2)).reshape(-1, DH),
        ],
        axis=0,
    )
    across = lax.ppermute(panel, "x_lo", [(0, 1), (1, 0)])
    far_mix = swapped(value_mix)
    both = packed(place, x, swapped(x))
    block, across = lax.optimization_barrier((block, across))
    low = lax.axis_index("x_lo") == 0
    pair = jnp.stack([jnp.where(low, panel, across), jnp.where(low, across, panel)])
    panels = lax.all_gather(pair, ("z", "core"), axis=0, tiled=False)
    mine, theirs = project(place, both, value_mix, far_mix, gathered(block))
    own = (mine + swapped(theirs)).astype(jnp.bfloat16)
    q = query(x, panels)

    other = lax.ppermute(own, "x_hi", [(0, 1), (1, 0)])
    own_1 = lax.ppermute(own, "y", [(0, 1), (1, 2), (2, 3)])
    own_3 = lax.ppermute(own, "y", [(0, 3)])
    own_2 = lax.ppermute(own, "y", [(0, 2), (1, 3)])
    other_1 = lax.ppermute(other, "y", [(0, 1), (1, 2), (2, 3)])
    other_3 = lax.ppermute(other, "y", [(0, 3)])
    other_2 = lax.ppermute(own_2, "x_hi", [(0, 1), (1, 0)])
    state = attend_early(
        place, q, [own, other, own_1, own_2, own_3], ((0, 0), (0, 1), (1, 0), (2, 0), (3, 0))
    )
    result = attend_late(
        place,
        q,
        state,
        output_mix,
        panels,
        [other_1, other_2, other_3],
        ((1, 0), (2, 0), (3, 0)),
    )
    return result[None]


def solution(mesh):
    grid = Mesh(mesh.devices.reshape(SIZES), AXES)
    seq = P(FSDP, CTX, None, None)
    in_specs = (
        P(FSDP, CTX, None),
        P(FSDP, None, None),
        P(FSDP, None, None),
        P(FSDP, None, None, None),
        P(None, None, None, FSDP),
        seq,
        seq,
        seq,
        seq,
    )
    return jax.shard_map(
        on_device, mesh=grid, in_specs=in_specs, out_specs=P(FSDP, CTX, None), check_vma=False
    )
```

```python
import functools
import itertools
import math

import jax
import jax.numpy as jnp
from jax import lax
from jax.experimental import pallas as pl
from jax.experimental.pallas import tpu as pltpu
from jax.sharding import Mesh
from jax.sharding import PartitionSpec as P

AXES = ("x_lo", "z", "core", "y", "x_hi")
SIZES = (2, 8, 2, 4, 2)
FSDP = ("x_lo", "z", "core")
CTX = ("y", "x_hi")
HEADS, EXPERTS, DH = 2, 4, 128
WIDTH = HEADS * DH
MIB = 1 << 20


def expert_mix(indices, gates):
    one_hot = (indices[..., None] == jnp.arange(EXPERTS, dtype=jnp.int32)).astype(jnp.float32)
    mix = jnp.sum(gates.astype(jnp.float32)[..., None] * one_hot, axis=-2)
    return mix.reshape(mix.shape[0], HEADS * EXPERTS).T


RING = 4
VM = pltpu.CompilerParams(vmem_limit_bytes=32 * MIB)


def moved(x, target):
    pairs = []
    for source, (x_lo, z, core, y, x_hi) in enumerate(itertools.product(*map(range, SIZES))):
        to_x, to_y, to_core = target(2 * x_hi + x_lo, y, core)
        to_x, to_y = to_x % RING, to_y % RING
        place = (((to_x % 2) * SIZES[1] + z) * SIZES[2] + to_core) * SIZES[3] + to_y
        pairs.append((source, place * SIZES[4] + to_x // 2))
    return lax.ppermute(x, AXES, pairs)


def hop(x, by, phase):
    return moved(
        x, lambda cx, cy, core: (cx + by, cy, core) if core == phase else (cx, cy + by, core)
    )


def swapped(x):
    return lax.ppermute(x, "core", [(0, 1), (1, 0)])


FIRST = ((0, -1), (1, 2))
GROUPS = ((0, 0), (0, 1), (-1, 0), (1, 1), (1, 0), (-1, 1), (2, 0), (2, 1))


def lifted(x):
    pairs = []
    for source, (x_lo, z, core, y, x_hi) in enumerate(itertools.product(*map(range, SIZES))):
        by = y * SIZES[4] + x_hi
        to_z = (z + by if core == 0 else z - by) % SIZES[1]
        place = ((x_lo * SIZES[1] + to_z) * SIZES[2] + core) * SIZES[3] + y
        pairs.append((source, place * SIZES[4] + x_hi))
    return lax.ppermute(x, AXES, pairs)


def gathered(block):
    up = hop(block, 1, 0)
    down = hop(block, -1, 0)
    across = hop(block, 2, 0)
    near = jnp.stack([block, up])
    far = jnp.stack([down, across])
    near_up = hop(near, 1, 1)
    far_down = hop(far, -1, 1)
    near_down = hop(near, -1, 1)
    far_up = hop(far, 1, 1)
    near_across = hop(near_up, 1, 1)
    far_across = hop(far_down, -1, 1)
    return [near, far, near_up, far_down, near_down, far_up, near_across, far_across]


def pack_kernel(place_ref, own_ref, other_ref, out_ref):
    rows = own_ref.shape[0]
    chip_x, chip_y, level, core = (place_ref[i] for i in range(4))
    for i, (second, pair) in enumerate(GROUPS):
        for j, first in enumerate(FIRST[pair]):
            by_x = jnp.where(core == 0, first, second)
            by_y = jnp.where(core == 0, second, first)
            from_x = lax.rem(chip_x + by_x + RING, RING)
            from_y = lax.rem(chip_y + by_y + RING, RING)
            by = from_y * SIZES[4] + lax.div(from_x, 2)
            from_z = lax.rem(level + jnp.where(core == 0, SIZES[1] - by, by), SIZES[1])
            shard = (lax.rem(from_x, 2) * SIZES[1] + from_z) * SIZES[2] + core
            lanes = pl.ds(pl.multiple_of(shard * DH, DH), DH)
            to = slice((2 * i + j) * DH, (2 * i + j + 1) * DH)
            out_ref[:rows, to] = own_ref[:, lanes]
            out_ref[rows:, to] = other_ref[:, lanes]


def packed(place, own, other):
    rows, depth = own.shape
    vmem = pl.BlockSpec(memory_space=pltpu.VMEM)
    return pl.pallas_call(
        pack_kernel,
        in_specs=[pl.BlockSpec(memory_space=pltpu.SMEM), vmem, vmem],
        out_specs=vmem,
        out_shape=jax.ShapeDtypeStruct((2 * rows, depth // 2), own.dtype),
        compiler_params=VM,
        cost_estimate=pl.CostEstimate(
            flops=0, bytes_accessed=6 * rows * depth, transcendentals=0
        ),
    )(place, own, other)


def project_kernel(count, place_ref, x_ref, mix_ref, far_mix_ref, *refs):
    pieces = refs[:count]
    outs = refs[count:]
    rows = outs[0].shape[0]
    mixes = (jnp.transpose(mix_ref[...]), jnp.transpose(far_mix_ref[...]))

    def product(column):
        w = jnp.concatenate(
            [piece[j, :, column : column + WIDTH] for piece in pieces for j in range(2)], axis=0
        )
        block = jnp.dot(x_ref[...], w, preferred_element_type=jnp.float32)
        return block[:rows], block[rows:]

    for out, block in zip(outs, product(0)):
        out[:, :WIDTH] = block
    for head in range(HEADS):
        for half in range(EXPERTS // 2):
            expert = head * EXPERTS + 2 * half
            lanes = slice(WIDTH + head * DH, WIDTH + (head + 1) * DH)
            for out, mix, block in zip(outs, mixes, product(WIDTH + expert * DH)):
                part = (
                    mix[:, expert : expert + 1] * block[:, :DH]
                    + mix[:, expert + 1 : expert + 2] * block[:, DH:]
                )
                out[:, lanes] = part if half == 0 else out[:, lanes] + part


def project(place, x, mix, far_mix, pieces):
    rows = x.shape[0] // 2
    depth = x.shape[1]
    _, shard, columns = pieces[0].shape
    vmem = pl.BlockSpec(memory_space=pltpu.VMEM)
    count = len(pieces)
    return pl.pallas_call(
        functools.partial(project_kernel, count),
        in_specs=[pl.BlockSpec(memory_space=pltpu.SMEM)] + [vmem] * (3 + count),
        out_specs=[vmem, vmem],
        out_shape=[jax.ShapeDtypeStruct((rows, 2 * WIDTH), jnp.float32)] * 2,
        compiler_params=VM,
        cost_estimate=pl.CostEstimate(
            flops=4 * rows * depth * columns,
            bytes_accessed=2 * depth * (2 * rows + columns),
            transcendentals=0,
        ),
    )(place, x, mix, far_mix, *pieces)


def query_kernel(x_ref, w_ref, q_ref, acc_ref):
    n = pl.program_id(0)
    count = w_ref.shape[0]
    w = jnp.concatenate(
        [
            jnp.concatenate([w_ref[i, :DH], w_ref[i, DH:]], axis=1)
            for i in range(count)
        ],
        axis=0,
    )
    part = jnp.dot(x_ref[...], w, preferred_element_type=jnp.float32)

    @pl.when(n == 0)
    def _():
        acc_ref[...] = part

    @pl.when(n > 0)
    def _():
        acc_ref[...] += part

    @pl.when(n == pl.num_programs(0) - 1)
    def _():
        q_ref[...] = acc_ref[...].astype(jnp.bfloat16)


def query(x, panels):
    rows, depth = x.shape
    shards = panels.shape[0] * panels.shape[1]
    steps = 4
    return pl.pallas_call(
        query_kernel,
        grid=(steps,),
        in_specs=[
            pl.BlockSpec((rows, depth // steps), lambda n: (0, n)),
            pl.BlockSpec((shards // steps, None, WIDTH, DH), lambda n: (n % 2, n // 2, 4, 0)),
        ],
        out_specs=pl.BlockSpec((rows, WIDTH), lambda n: (0, 0)),
        out_shape=jax.ShapeDtypeStruct((rows, WIDTH), jnp.bfloat16),
        scratch_shapes=[pltpu.VMEM((rows, WIDTH), jnp.float32)],
        compiler_params=VM,
        cost_estimate=pl.CostEstimate(
            flops=2 * rows * depth * WIDTH,
            bytes_accessed=2 * (rows * depth + depth * WIDTH),
            transcendentals=0,
        ),
    )(x, panels)


LOG2E = 1.4426950408889634
PANELS = 4


def attend_block(q_ref, kv, m_ref, l_ref, acc_ref, diagonal):
    scale = LOG2E / math.sqrt(DH)
    for head in range(HEADS):
        lanes = slice(head * DH, (head + 1) * DH)
        one = slice(head, head + 1)
        keys, mixed, shift = (kv[0], kv[1], 0) if isinstance(kv, tuple) else (kv, kv, WIDTH)
        scores = lax.dot_general(
            keys[:, lanes],
            q_ref[:, lanes],
            (((1,), (1,)), ((), ())),
            preferred_element_type=jnp.float32,
        )
        values = mixed[:, shift + head * DH : shift + (head + 1) * DH]
        if diagonal:
            k_pos = lax.broadcasted_iota(jnp.int32, scores.shape, 0)
            q_pos = lax.broadcasted_iota(jnp.int32, scores.shape, 1)
            scores = jnp.where(q_pos >= k_pos, scores, -jnp.inf)
            top = jnp.max(scores, axis=0, keepdims=True)
        else:
            before = m_ref[one]
            top = jnp.maximum(before, jnp.max(scores, axis=0, keepdims=True))
            rescale = jnp.exp2((before - top) * scale)
        weights = jnp.exp2((scores - top) * scale)
        total = jnp.sum(weights, axis=0, keepdims=True)
        update = lax.dot_general(
            values,
            weights.astype(jnp.bfloat16),
            (((0,), (0,)), ((), ())),
            preferred_element_type=jnp.float32,
        )
        m_ref[one] = top
        if diagonal:
            l_ref[one] = total
            acc_ref[lanes] = update
        else:
            l_ref[one] = l_ref[one] * rescale + total
            acc_ref[lanes] = acc_ref[lanes] * rescale + update


def attend_blocks(place_ref, needs, diagonal, q_ref, kv_refs, *state):
    row, side = place_ref[1], lax.div(place_ref[0], 2)
    for k, kv in enumerate(kv_refs):
        if diagonal and k == 0:
            attend_block(q_ref, kv, *state, True)
        else:
            pl.when((row >= needs[k][0]) & (side >= needs[k][1]))(
                functools.partial(attend_block, q_ref, kv, *state, False)
            )


def attend_early_kernel(needs, place_ref, q_ref, *refs):
    count = len(needs)
    attend_blocks(place_ref, needs, True, q_ref, refs[:count], *refs[count:])


def attend_late_kernel(needs, place_ref, q_ref, m_in, l_in, acc_in, mix_ref, panels, *refs):
    count = len(needs) + 1
    blocks = ((refs[0], refs[1]),) + refs[2:count]
    out_hbm = refs[count]
    m_ref, l_ref, acc_ref, mixed_ref, w_ref, o_ref, w_sem, o_sem = refs[count + 1 :]
    depth = mixed_ref.shape[1]
    levels, lows = panels.shape[:2]
    w_copies = [
        pltpu.make_async_copy(
            panels.at[pl.ds(first, PANELS), low, pl.ds(0, depth)],
            w_ref.at[pl.ds(low * levels + first, PANELS)],
            w_sem,
        )
        for low in range(lows)
        for first in range(0, levels, PANELS)
    ]
    for copy in w_copies:
        copy.start()
    m_ref[...] = m_in[...]
    l_ref[...] = l_in[...]
    acc_ref[...] = acc_in[...]
    attend_blocks(place_ref, needs, False, q_ref, blocks, m_ref, l_ref, acc_ref)
    mix = jnp.transpose(mix_ref[...])
    for head in range(HEADS):
        attended = acc_ref[head * DH : (head + 1) * DH] / l_ref[head : head + 1]
        attended = jnp.transpose(attended).astype(jnp.bfloat16).astype(jnp.float32)
        for expert in range(EXPERTS):
            index = head * EXPERTS + expert
            mixed_ref[:, index * DH : (index + 1) * DH] = (
                mix[:, index : index + 1] * attended
            ).astype(jnp.bfloat16)
    for copy in w_copies:
        copy.wait()
    o_copies = []
    width = 2 * DH
    for i in range(0, levels * lows, 2):
        panel = jnp.concatenate([w_ref[i], w_ref[i + 1]], axis=1)
        block = jnp.dot(mixed_ref[...], panel, preferred_element_type=jnp.float32)
        o_ref[:, i * DH : i * DH + width] = block.astype(jnp.bfloat16)
        if i % PANELS == PANELS - 2:
            lanes = pl.ds((i + 2 - PANELS) * DH, PANELS * DH)
            o_copies.append(
                pltpu.make_async_copy(o_ref.at[:, lanes], out_hbm.at[:, lanes], o_sem)
            )
            o_copies[-1].start()
    for copy in o_copies:
        copy.wait()


def state_shapes(rows):
    return [(HEADS, rows), (HEADS, rows), (WIDTH, rows)]


def attend_cost(rows, count, flops):
    return pl.CostEstimate(
        flops=4 * rows * rows * DH * HEADS * count + flops,
        bytes_accessed=2 * rows * WIDTH * 2 * count,
        transcendentals=rows * rows * HEADS * count,
    )


def attend_early(place, q, blocks, needs):
    rows = q.shape[0]
    vmem = pl.BlockSpec(memory_space=pltpu.VMEM)
    return pl.pallas_call(
        functools.partial(attend_early_kernel, needs),
        in_specs=[pl.BlockSpec(memory_space=pltpu.SMEM)] + [vmem] * (1 + len(blocks)),
        out_specs=[vmem] * 3,
        out_shape=[jax.ShapeDtypeStruct(s, jnp.float32) for s in state_shapes(rows)],
        compiler_params=VM,
        cost_estimate=attend_cost(rows, len(blocks), 0),
    )(place, q, *blocks)


def attend_late(place, q, state, mix, panels, blocks, needs):
    rows = q.shape[0]
    depth = HEADS * EXPERTS * DH
    levels, lows, _, width = panels.shape
    columns = levels * lows * width
    vmem = pl.BlockSpec(memory_space=pltpu.VMEM)
    any_space = pl.BlockSpec(memory_space=pl.ANY)
    return pl.pallas_call(
        functools.partial(attend_late_kernel, needs),
        in_specs=[pl.BlockSpec(memory_space=pltpu.SMEM)]
        + [vmem] * 5
        + [any_space]
        + [vmem] * len(blocks),
        out_specs=any_space,
        out_shape=jax.ShapeDtypeStruct((rows, columns), jnp.bfloat16),
        scratch_shapes=[pltpu.VMEM(s, jnp.float32) for s in state_shapes(rows)]
        + [
            pltpu.VMEM((rows, depth), jnp.bfloat16),
            pltpu.VMEM((levels * lows, depth, width), jnp.bfloat16),
            pltpu.VMEM((rows, columns), jnp.bfloat16),
            pltpu.SemaphoreType.DMA,
            pltpu.SemaphoreType.DMA,
        ],
        compiler_params=VM,
        cost_estimate=attend_cost(rows, len(blocks), 2 * rows * depth * columns),
    )(place, q, *state, mix, panels, *blocks)


def on_device(
    tokens, w_query, w_key, w_value, w_out, value_experts, value_gates, output_experts, output_gates
):
    x = tokens[0]
    y, x_hi = lax.axis_index("y"), lax.axis_index("x_hi")
    chip_x = 2 * x_hi + lax.axis_index("x_lo")
    place = jnp.stack([chip_x, y, lax.axis_index("z"), lax.axis_index("core")]).astype(jnp.int32)
    shard = w_key.shape[0]
    block = lifted(
        jnp.concatenate([w_key.reshape(shard, -1), w_value.reshape(shard, -1)], axis=1)
    )
    value_mix = expert_mix(value_experts[0], value_gates[0])
    output_mix = expert_mix(output_experts[0], output_gates[0])
    output_mix = output_mix.astype(jnp.bfloat16).astype(jnp.float32)
    panel = jnp.concatenate(
        [
            w_out.reshape(-1, w_out.shape[3]),
            jnp.transpose(w_query, (1, 0, 2)).reshape(-1, DH),
        ],
        axis=0,
    )
    across = lax.ppermute(panel, "x_lo", [(0, 1), (1, 0)])
    far_mix = swapped(value_mix)
    both = packed(place, x, swapped(x))
    block, across = lax.optimization_barrier((block, across))
    low = lax.axis_index("x_lo") == 0
    pair = jnp.stack([jnp.where(low, panel, across), jnp.where(low, across, panel)])
    panels = lax.all_gather(pair, ("z", "core"), axis=0, tiled=False)
    mine, theirs = project(place, both, value_mix, far_mix, gathered(block))
    own = (mine + swapped(theirs)).astype(jnp.bfloat16)
    q = query(x, panels)

    other = lax.ppermute(own, "x_hi", [(0, 1), (1, 0)])
    own_1 = lax.ppermute(own, "y", [(0, 1), (1, 2), (2, 3)])
    own_3 = lax.ppermute(own, "y", [(0, 3)])
    own_2 = lax.ppermute(own, "y", [(0, 2), (1, 3)])
    other_1k = lax.ppermute(other[:, :WIDTH], "y", [(0, 1), (1, 2), (2, 3)])
    other_1v = lax.ppermute(own_1[:, WIDTH:], "x_hi", [(0, 1), (1, 0)])
    other_3 = lax.ppermute(other, "y", [(0, 3)])
    other_2 = lax.ppermute(own_2, "x_hi", [(0, 1), (1, 0)])
    state = attend_early(
        place, q, [own, other, own_1, own_2, own_3], ((0, 0), (0, 1), (1, 0), (2, 0), (3, 0))
    )
    result = attend_late(
        place,
        q,
        state,
        output_mix,
        panels,
        [other_1k, other_1v, other_2, other_3],
        ((1, 0), (2, 0), (3, 0)),
    )
    return result[None]


def solution(mesh):
    grid = Mesh(mesh.devices.reshape(SIZES), AXES)
    seq = P(FSDP, CTX, None, None)
    in_specs = (
        P(FSDP, CTX, None),
        P(FSDP, None, None),
        P(FSDP, None, None),
        P(FSDP, None, None, None),
        P(None, None, None, FSDP),
        seq,
        seq,
        seq,
        seq,
    )
    return jax.shard_map(
        on_device, mesh=grid, in_specs=in_specs, out_specs=P(FSDP, CTX, None), check_vma=False
    )
```
